32 devices in a mesh: tile: 8 (over y, x, core), phi: 4 (over z).
Axes of the slice: x: 2, y: 2, z: 4, core: 2. Of those that a mesh axis runs over, the one named last changes fastest.
Arguments:
- blocks: bfloat16 [2048, 5, 64, 256], P(('tile', 'phi')), may hold values from -6 to 6
- levels: int32 [2048], P(('tile', 'phi')), may hold values from 0 to 3
- block_dest: int32 [2048], P(('tile', 'phi')), may hold values from 0 to 7, as said below
- block_phi: int32 [2048], P(('tile', 'phi')), may hold values from 0 to 7, as said below
- block_group: int32 [2048], P(('tile', 'phi')), may hold values from 0 to 7, as said below
Outputs:
- spectra: float32 [5, 64, 256, 2048], P(None, 'tile', 'phi')
The draws below stay inside these ranges and needn't reach their ends.
Inputs may be any that keep to these rules, and one draw needn't show every extreme that they name: `block_dest`: at most 16 of one device's blocks name one tile, and some device sends exactly 16 to some tile; for each tile and each phi segment, the blocks of that segment that name the tile are exactly 64. Among the blocks of one phi segment that name one tile, the pairs (block_phi, block_group) take each of the 64 values once. `block_group`: see block_phi.
All inputs are finite; a program needn't handle non-finite values.
Results may differ from the reference program's by a relative error of at most 0.003.
Values may be sent and summed in bfloat16 or wider, within the bound.
No kernel may reach another device: no remote copies, remote signals or barrier semaphores. Data moves between devices by JAX's collectives and lax.ppermute only.
A program may use at most 192 MiB of HBM per device.

```python
import math
import jax
import jax.numpy as jnp
from jax import lax

FIELDS = 5
NPHI = 2048
BPHI = 64
COLS = 256
CG_DEV = 8
LEVELS = 4
PHIBLK = 32
PB_DEV = 8
SLOTS = 64
NB = 2048
NCG = 64
N_TILE = 8
N_PHI = 4


def block_layout(key):
    base = jax.random.fold_in(key, 11)
    keys = jax.random.split(base, 5)
    tile_count = N_TILE
    plane_count = N_PHI
    device_count = tile_count * plane_count
    average = SLOTS // tile_count

    def plane_counts(plane_key):
        order_key, delta_key = jax.random.split(plane_key)
        order = jax.random.permutation(order_key, tile_count)
        deltas = jax.random.randint(delta_key, (tile_count // 2,), 0, average + 1).at[0].set(average)
        counts = jnp.zeros((tile_count,), jnp.int32)
        counts = counts.at[order[0::2]].set(average + deltas)
        counts = counts.at[order[1::2]].set(average - deltas)
        return counts
    counts = jax.vmap(plane_counts)(jax.random.split(keys[0], plane_count))
    rho = jax.vmap(lambda kk: jax.random.permutation(kk, tile_count))(jax.random.split(keys[1], plane_count))
    tau = jax.vmap(lambda kk: jax.random.permutation(kk, tile_count))(jax.random.split(keys[2], plane_count))
    shift_table = jax.vmap(lambda cc: jnp.repeat(jnp.arange(tile_count, dtype=jnp.int32), cc, total_repeat_length=SLOTS))(counts)
    slot_perms = jax.vmap(lambda kk: jax.random.permutation(kk, SLOTS))(jax.random.split(keys[3], device_count))
    source = jnp.arange(device_count, dtype=jnp.int32)
    source_tile = source // plane_count
    source_plane = source % plane_count
    shifts = shift_table[source_plane[:, None], slot_perms]
    dest = rho[source_plane[:, None], (tau[source_plane, source_tile][:, None] + shifts) % tile_count]
    plane_full = jnp.broadcast_to(source_plane[:, None], (device_count, SLOTS))
    receiver = (dest * plane_count + plane_full).reshape(NB)
    onehot_dest = (receiver[:, None] == jnp.arange(device_count, dtype=jnp.int32)[None, :]).astype(jnp.int32)
    arrival = jnp.sum((jnp.cumsum(onehot_dest, axis=0) - 1) * onehot_dest, axis=1)
    place_perms = jax.vmap(lambda kk: jax.random.permutation(kk, SLOTS))(jax.random.split(keys[4], device_count))
    position = place_perms[receiver, arrival]
    return (dest.reshape(NB).astype(jnp.int32), (position // CG_DEV).astype(jnp.int32), (position % CG_DEV).astype(jnp.int32))


def draw_block_dest(key, part):
    return block_layout(key)[0]


def draw_block_phi(key, part):
    return block_layout(key)[1]


def draw_block_group(key, part):
    return block_layout(key)[2]


def set_ends(values, rng, least, top_value):
    longest = values.shape.index(max(values.shape))
    spots = []
    for shift in (0, 1):
        where = [jax.random.randint(jax.random.fold_in(rng, axis), (), 0, length) for axis, length in enumerate(values.shape)]
        where[longest] = (where[longest] + shift) % values.shape[longest]
        spots.append(tuple(where))
    return values.at[spots[0]].set(least).at[spots[1]].set(top_value)


def block_scale(own_key, extent, cuts, least, largest):
    level = 1.0
    for dim, parts in cuts:
        steps = jax.random.uniform(jax.random.fold_in(jax.random.fold_in(own_key, 6), dim), (parts,), jnp.float32, least / len(cuts), largest / len(cuts))
        level = level * jnp.repeat(jnp.exp(steps), extent[dim] // parts).reshape((-1,) + (1,) * (len(extent) - 1 - dim))
    return level


def centred(stream_key, shape, deviation, bound, pieces=(), held_as=jnp.bfloat16):
    entries = jax.random.normal(stream_key, shape, jnp.float32) * deviation
    if len(pieces) > 0:
        entries = block_scale(stream_key, shape, pieces, -0.22, 0.18) * entries
    return jnp.clip(entries, min=-bound, max=bound).astype(held_as)


def setup_inputs(seed: int = 0) -> dict:
    splits = jax.random.split(jax.random.key(seed), 6)
    blocks = centred(splits[0], (NB, FIELDS, BPHI, COLS), 1.0, 6.0, ((0, 32),))
    levels = set_ends(jax.random.randint(splits[1], (NB,), 0, LEVELS), jax.random.fold_in(splits[1], 1), 0, LEVELS - 1).astype(jnp.int32)
    block_dest = draw_block_dest(jax.random.fold_in(splits[5], 71), 0)
    block_phi = draw_block_phi(jax.random.fold_in(splits[5], 71), 0)
    block_group = draw_block_group(jax.random.fold_in(splits[5], 71), 0)
    return {"blocks": blocks, "levels": levels, "block_dest": block_dest, "block_phi": block_phi, "block_group": block_group}


def dft_basis(length):
    column = jnp.arange(length, dtype=jnp.int32)
    half = length // 2
    mode = jnp.where(column <= half, column, column - half)
    phase = column[:, None] * mode[None, :] % length
    angle = phase.astype(jnp.float32) * jnp.float32(2.0 * math.pi / length)
    values = jnp.where((column <= half)[None, :], jnp.cos(angle), jnp.sin(angle))
    return (values * jnp.float32(1.0 / math.sqrt(length))).astype(jnp.bfloat16)

def reference(blocks, levels, block_dest, block_phi, block_group):
    weight = (1.0 / jnp.left_shift(1, levels).astype(jnp.float32)).astype(jnp.bfloat16)
    weighted = blocks * weight[:, None, None, None]
    index_all = jnp.arange(NB, dtype=jnp.int32)
    segment = index_all // SLOTS % N_PHI
    global_phi = (segment * PB_DEV + block_phi).astype(jnp.int32)
    global_group = (block_dest * CG_DEV + block_group).astype(jnp.int32)
    field = jnp.zeros((PHIBLK, NCG, FIELDS, BPHI, COLS), jnp.bfloat16)
    field = field.at[global_phi, global_group].set(weighted)
    basis_table = dft_basis(NPHI).astype(jnp.float32)

    def one_group(group_index):
        column_block = field[:, group_index]
        column_block = jnp.transpose(column_block, (1, 0, 2, 3)).reshape(FIELDS, NPHI, COLS)
        return jnp.einsum('fpc,pk->fck', column_block.astype(jnp.float32), basis_table, precision=lax.Precision.HIGHEST)
    stacked = lax.map(one_group, jnp.arange(NCG, dtype=jnp.int32))
    return jnp.transpose(stacked, (1, 0, 2, 3))
```

```python
import functools
import math

import jax
import jax.numpy as jnp
from jax import lax
from jax.experimental import pallas as pl
from jax.experimental.pallas import tpu as pltpu
from jax.sharding import PartitionSpec as P

FIELDS = 5
NPHI = 2048
BPHI = 64
COLS = 256
CG_DEV = 8
LANES = 128
FIRST = 2
VMEM_BYTES = 48 * 1024 * 1024

ANY = pl.BlockSpec(memory_space=pl.ANY)
SMEM = pl.BlockSpec(memory_space=pltpu.SMEM)
VMEM = pl.BlockSpec(memory_space=pltpu.VMEM)


def rotated_basis(length, start):
    row = start
    column = jnp.arange(length, dtype=jnp.int32)
    half = length // 2
    mode = jnp.where(column <= half, column, column - half)
    phase = row[:, None] * mode[None, :] % length
    angle = phase.astype(jnp.float32) * jnp.float32(2.0 * math.pi / length)
    values = jnp.where((column <= half)[None, :], jnp.cos(angle), jnp.sin(angle))
    return (values * jnp.float32(1.0 / math.sqrt(length))).astype(jnp.bfloat16)


def granules(block, planes):
    turned = block.T
    sliver = COLS // planes
    half = sliver // 2
    out = []
    for p in range(planes):
        low = turned[p * sliver : p * sliver + half]
        high = turned[p * sliver + half : (p + 1) * sliver]
        out.append(jnp.concatenate([low, high], axis=1))
    return out


def params(**kw):
    return pltpu.CompilerParams(vmem_limit_bytes=VMEM_BYTES, **kw)


def cut_kernel(planes, chunk, count, me_ref, weight_ref, x_ref, *outs):
    base = pl.program_id(0) * chunk
    me = me_ref[0]
    for mine in range(planes):

        @pl.when(me == mine)
        def _():
            def body(i, carry):
                w = weight_ref[base + i]
                for f in range(count):
                    x = (x_ref[i, f].astype(jnp.float32) * w).astype(jnp.bfloat16)
                    for p, g in enumerate(granules(x, planes)):
                        outs[(p - mine) % planes][f, i] = g
                return carry

            lax.fori_loop(0, chunk, body, 0)


def cut(blocks, weight, me, planes, count):
    slots = blocks.shape[0]
    chunk = 8
    half = COLS // planes // 2
    return pl.pallas_call(
        functools.partial(cut_kernel, planes, chunk, count),
        grid=(slots // chunk,),
        in_specs=[
            SMEM,
            SMEM,
            pl.BlockSpec((chunk, count, BPHI, COLS), lambda i: (i, 0, 0, 0)),
        ],
        out_specs=[pl.BlockSpec((count, chunk, half, LANES), lambda i: (0, i, 0, 0))] * planes,
        out_shape=[jax.ShapeDtypeStruct((count, slots, half, LANES), jnp.bfloat16)] * planes,
        compiler_params=params(),
        name="cut",
    )(me, weight, blocks)


def post_kernel(fields, slot_ref, x_ref, *rest):
    outs, sems = rest[:-1], rest[-1]
    slots = slot_ref.shape[0]
    for k, f in enumerate(fields):

        def body(i, carry):
            pltpu.make_async_copy(x_ref.at[i, f], outs[k].at[slot_ref[i]], sems.at[k]).start()
            return carry

        lax.fori_loop(0, slots, body, 0)
    for k, f in enumerate(fields):
        part = outs[k].at[pl.ds(0, slots)]
        pltpu.make_async_copy(part, part, sems.at[k]).wait()


def post(blocks, slot, fields, room):
    return pl.pallas_call(
        functools.partial(post_kernel, fields),
        in_specs=[SMEM, ANY],
        out_specs=[ANY] * len(fields),
        out_shape=[jax.ShapeDtypeStruct((room, BPHI, COLS), jnp.bfloat16)] * len(fields),
        scratch_shapes=[pltpu.SemaphoreType.DMA((len(fields),))],
        compiler_params=params(),
        name="post",
    )(slot, blocks)


def sort_kernel(planes, me_ref, slot_ref, weight_ref, x_ref, *rest):
    outs, (buf, sem) = rest[:planes], rest[planes:]
    places = slot_ref.shape[0]
    me = me_ref[0]

    def fetch(i, carry):
        pltpu.make_async_copy(x_ref.at[slot_ref[i]], buf.at[i], sem).start()
        return carry

    lax.fori_loop(0, places, fetch, 0)
    pltpu.make_async_copy(buf, buf, sem).wait()
    for mine in range(planes):

        @pl.when(me == mine)
        def _():
            def body(i, carry):
                x = (buf[i].astype(jnp.float32) * weight_ref[i]).astype(jnp.bfloat16)
                for p, g in enumerate(granules(x, planes)):
                    outs[(p - mine) % planes][i] = g
                return carry

            lax.fori_loop(0, places, body, 0)


def sort(arrived, slot, weight, me, planes):
    places = slot.shape[0]
    half = COLS // planes // 2
    return pl.pallas_call(
        functools.partial(sort_kernel, planes),
        in_specs=[SMEM, SMEM, SMEM, ANY],
        out_specs=[VMEM] * planes,
        out_shape=[jax.ShapeDtypeStruct((places, half, LANES), jnp.bfloat16)] * planes,
        scratch_shapes=[
            pltpu.VMEM((places, BPHI, COLS), jnp.bfloat16),
            pltpu.SemaphoreType.DMA,
        ],
        compiler_params=params(),
        name="sort",
    )(me, slot, weight, arrived)


def mail_kernel(planes, count, slot_ref, *rest):
    ins, outs, sems = rest[:planes], rest[planes : planes + count], rest[-1]
    slots = slot_ref.shape[1]
    for f in range(count):
        for d in range(planes):

            def body(i, carry):
                pltpu.make_async_copy(
                    ins[d].at[f, i], outs[f].at[slot_ref[d, i]], sems.at[f, d]
                ).start()
                return carry

            lax.fori_loop(0, slots, body, 0)
    for f in range(count):
        for d in range(planes):
            part = outs[f].at[pl.ds(0, slots)]
            pltpu.make_async_copy(part, part, sems.at[f, d]).wait()


def mail(parts, slot, room):
    planes = len(parts)
    count, _, half, _ = parts[0].shape
    return pl.pallas_call(
        functools.partial(mail_kernel, planes, count),
        in_specs=[SMEM] + [ANY] * planes,
        out_specs=[ANY] * count,
        out_shape=[jax.ShapeDtypeStruct((room, half, LANES), jnp.bfloat16)] * count,
        scratch_shapes=[pltpu.SemaphoreType.DMA((count, planes))],
        compiler_params=params(),
        name="mail",
    )(slot, *parts)


def transform_kernel(planes, field, routed, chained, *refs):
    refs = list(refs)
    slot_ref = refs.pop(0) if routed else None
    ins = [refs.pop(0)] if routed else [refs.pop(0) for _ in range(planes)]
    basis_hbm = refs.pop(0)
    if chained:
        refs.pop(0)
    out_hbm, gran, rows, basis, acc, in_sems, basis_sems, out_sems = refs
    per_plane = gran.shape[1]
    half = gran.shape[3]
    chunks = basis_sems.shape[0]
    wide = NPHI // chunks

    for j in range(chunks):
        span = pl.ds(j * wide, wide)
        pltpu.make_async_copy(basis_hbm.at[:, span], basis.at[j], basis_sems.at[j]).start()
    for d in range(planes):
        if routed:

            def fetch(i, carry):
                a, b = i // CG_DEV, i % CG_DEV
                pltpu.make_async_copy(
                    ins[0].at[slot_ref[d, i]], gran.at[d, a, b], in_sems.at[d]
                ).start()
                return carry

            lax.fori_loop(0, per_plane * CG_DEV, fetch, 0)
        else:
            pltpu.make_async_copy(ins[d], gran.at[d], in_sems.at[d]).start()
    low = lax.broadcasted_iota(jnp.int32, (half, LANES), 1) < BPHI
    for d in range(planes):
        pltpu.make_async_copy(gran.at[d], gran.at[d], in_sems.at[d]).wait()
        for j in range(per_plane // 2):
            for g in range(CG_DEV):
                even = gran[d, 2 * j, g]
                odd = gran[d, 2 * j + 1, g]
                first = jnp.concatenate([even[:, :BPHI], odd[:, :BPHI]], axis=1)
                second = jnp.concatenate([even[:, BPHI:], odd[:, BPHI:]], axis=1)
                lanes = pl.ds((d * per_plane + 2 * j) * BPHI, LANES)
                rows[pl.ds(2 * g * half, half), lanes] = first
                rows[pl.ds((2 * g + 1) * half, half), lanes] = second
    copies = []
    for j in range(chunks):
        pltpu.make_async_copy(basis.at[j], basis.at[j], basis_sems.at[j]).wait()
        if j >= 2:
            copies[j - 2].wait()
        acc[j % 2] = jnp.dot(rows[...], basis[j], preferred_element_type=jnp.float32).reshape(
            acc.shape[1:]
        )
        copy = pltpu.make_async_copy(
            acc.at[j % 2], out_hbm.at[field, :, :, pl.ds(j * wide, wide)], out_sems.at[j]
        )
        copy.start()
        copies.append(copy)
    for copy in copies[-2:]:
        copy.wait()


def transform(inputs, slot, basis, total, field, planes, per_plane):
    sliver = COLS // planes
    chunks = 4
    routed = slot is not None
    operands = ([slot] if routed else []) + list(inputs) + [basis]
    specs = ([SMEM] if routed else []) + [ANY] * (len(inputs) + 1)
    aliases = {}
    if total is not None:
        aliases = {len(operands): 0}
        operands.append(total)
        specs.append(ANY)
    wide = NPHI // chunks
    return pl.pallas_call(
        functools.partial(transform_kernel, planes, field, routed, total is not None),
        in_specs=specs,
        out_specs=ANY,
        out_shape=jax.ShapeDtypeStruct((FIELDS, CG_DEV, sliver, NPHI), jnp.float32),
        scratch_shapes=[
            pltpu.VMEM((planes, per_plane, CG_DEV, sliver // 2, LANES), jnp.bfloat16),
            pltpu.VMEM((CG_DEV * sliver, NPHI), jnp.bfloat16),
            pltpu.VMEM((chunks, NPHI, wide), jnp.bfloat16),
            pltpu.VMEM((2, CG_DEV, sliver, wide), jnp.float32),
            pltpu.SemaphoreType.DMA((planes,)),
            pltpu.SemaphoreType.DMA((chunks,)),
            pltpu.SemaphoreType.DMA((chunks,)),
        ],
        input_output_aliases=aliases,
        compiler_params=params(),
        name="transform",
    )(*operands)


def rank_of(dest):
    slots = dest.shape[-1]
    at = jnp.arange(slots, dtype=jnp.int32)
    same = (dest[..., :, None] == dest[..., None, :]) & (at[None, :] < at[:, None])
    return jnp.sum(same.astype(jnp.int32), axis=-1)


def local(blocks, levels, block_dest, block_phi, block_group):
    tiles = lax.axis_size("tile")
    planes = lax.axis_size("phi")
    tile = lax.axis_index("tile")
    plane = lax.axis_index("phi")
    slots = blocks.shape[0]
    per_plane = NPHI // BPHI // planes
    places = per_plane * CG_DEV
    capacity = 2 * slots // tiles
    me = plane.astype(jnp.int32).reshape(1)
    weight = 1.0 / jnp.left_shift(1, levels).astype(jnp.float32)

    def over_phi(parts):
        moved = [parts[0]]
        for d in range(1, planes):
            pairs = [(s, (s + d) % planes) for s in range(planes)]
            moved.append(lax.ppermute(parts[d], "phi", pairs))
        return moved

    def over_tile(box):
        return lax.all_to_all(box, "tile", split_axis=0, concat_axis=0, tiled=True)

    code = ((levels * tiles + block_dest) * per_plane + block_phi) * CG_DEV + block_group
    codes = lax.all_gather(code, ("tile", "phi"), axis=0, tiled=True)
    codes = codes.reshape(tiles, planes, slots)

    own_rank = rank_of(block_dest)
    later = tuple(range(FIRST, FIELDS))
    boxes = post(blocks, block_dest * capacity + own_rank, later, tiles * capacity)
    pieces = cut(blocks, weight, me, planes, FIRST)

    back = (plane - jnp.arange(planes, dtype=jnp.int32)) % planes
    near = jnp.take(codes, back, axis=1)
    dest = near // places % tiles
    rank = rank_of(dest)
    level = near // (places * tiles)
    here = (dest == tile)[..., None] & (
        (near % places)[..., None] == jnp.arange(places, dtype=jnp.int32)
    )
    from_tile = jnp.arange(tiles, dtype=jnp.int32)[:, None, None]
    distance = jnp.arange(planes, dtype=jnp.int32)[None, :, None]
    routed = (from_tile * planes + distance) * capacity + rank
    routed = jnp.sum(jnp.where(here, routed[..., None], 0), axis=(0, 2))
    arrived = from_tile[:, 0] * capacity + rank[:, 0]
    arrived = jnp.sum(jnp.where(here[:, 0], arrived[..., None], 0), axis=(0, 1))
    arrived_level = jnp.sum(jnp.where(here[:, 0], level[:, 0, :, None], 0), axis=(0, 1))
    arrived_weight = 1.0 / jnp.left_shift(1, arrived_level).astype(jnp.float32)
    out_dest = lax.dynamic_index_in_dim(dest, tile, 0, keepdims=False)
    out_rank = lax.dynamic_index_in_dim(rank, tile, 0, keepdims=False)
    out_slot = (out_dest * planes + distance[0]) * capacity + out_rank

    cell = jnp.arange(per_plane * BPHI, dtype=jnp.int32)
    basis = rotated_basis(NPHI, (back[:, None] * (per_plane * BPHI) + cell[None, :]).reshape(NPHI))

    sent = over_phi(pieces)
    outboxes = None
    parts = {}
    for f, box in zip(later, boxes):
        parts[f] = over_phi(sort(over_tile(box), arrived, arrived_weight, me, planes))
    outboxes = mail(sent, out_slot, tiles * planes * capacity)
    for f in range(FIRST):
        parts[f] = over_tile(outboxes[f])
    total = None
    for f in [2, 0, 3, 1, 4]:
        got = parts[f]
        if f < FIRST:
            total = transform([got], routed, basis, total, f, planes, per_plane)
        else:
            got = [g.reshape(per_plane, CG_DEV, *g.shape[1:]) for g in got]
            total = transform(got, None, basis, total, f, planes, per_plane)
    return total


def solution(mesh):
    in_specs = (
        P(("tile", "phi"), None, None, None),
        P(("tile", "phi")),
        P(("tile", "phi")),
        P(("tile", "phi")),
        P(("tile", "phi")),
    )
    out_specs = P(None, "tile", "phi", None)
    return jax.shard_map(local, mesh=mesh, in_specs=in_specs, out_specs=out_specs, check_vma=False)
```

```python
import functools
import math

import jax
import jax.numpy as jnp
from jax import lax
from jax.experimental import pallas as pl
from jax.experimental.pallas import tpu as pltpu
from jax.sharding import PartitionSpec as P

FIELDS = 5
NPHI = 2048
BPHI = 64
COLS = 256
CG_DEV = 8
LANES = 128
NOTE = 16
PAIR = (0, 1)
GROUPS = ((2, 3), (4,))
VMEM_BYTES = 32 * 1024 * 1024
SPANS = 4
LIGHT = pl.CostEstimate(flops=0, bytes_accessed=0, transcendentals=0)

ANY = pl.BlockSpec(memory_space=pl.ANY)
HBM = pl.BlockSpec(memory_space=pltpu.HBM)
SMEM = pl.BlockSpec(memory_space=pltpu.SMEM)
VMEM = pl.BlockSpec(memory_space=pltpu.VMEM)


def rotated_basis(length, back):
    planes = back.shape[0]
    per = length // planes
    column = jnp.arange(length, dtype=jnp.int32)
    half = length // 2
    mode = jnp.where(column <= half, column, column - half)
    coarse = (back[:, None] * per + jnp.arange(0, per, BPHI, dtype=jnp.int32)[None, :]).reshape(-1)
    fine = jnp.arange(BPHI, dtype=jnp.int32)

    def angle(row):
        phase = row[:, None] * mode[None, :] % length
        return phase.astype(jnp.float32) * jnp.float32(2.0 * math.pi / length)

    even = (column <= half)[None, :]
    scale = jnp.float32(1.0 / math.sqrt(length))
    far, near = angle(coarse), angle(fine)
    by_cos = jnp.where(even, jnp.cos(far), jnp.sin(far)) * scale
    by_sin = jnp.where(even, -jnp.sin(far), jnp.cos(far)) * scale
    near_cos, near_sin = jnp.cos(near), jnp.sin(near)

    def spans(x):
        return x.reshape(x.shape[0], SPANS, length // SPANS).transpose(1, 0, 2)

    by_cos, by_sin = spans(by_cos)[:, :, None], spans(by_sin)[:, :, None]
    near_cos, near_sin = spans(near_cos)[:, None], spans(near_sin)[:, None]
    by_cos, by_sin, near_cos, near_sin = lax.optimization_barrier((by_cos, by_sin, near_cos, near_sin))
    table = by_cos * near_cos + by_sin * near_sin
    return table.reshape(SPANS, length, length // SPANS).astype(jnp.bfloat16)


def in_hbm(*arrays):
    return [pltpu.with_memory_space_constraint(a, pltpu.HBM) for a in arrays]


def params():
    return pltpu.CompilerParams(vmem_limit_bytes=VMEM_BYTES)


def scaled(block, weight):
    return block * jnp.full((1, 1), weight, jnp.float32).astype(jnp.bfloat16)


def cut_kernel(planes, chunk, me_ref, weight_ref, x_ref, *outs):
    base = pl.program_id(0) * chunk
    sliver = COLS // planes
    for mine in range(planes):

        @pl.when(me_ref[0] == mine)
        def _():
            def body(i, carry):
                x = scaled(x_ref[i].reshape(LANES, COLS), weight_ref[base + i]).T
                for p in range(planes):
                    outs[(p - mine) % planes][i] = x[p * sliver : (p + 1) * sliver]
                return carry

            lax.fori_loop(0, chunk, body, 0, unroll=4)


def cut(blocks, weight, me, planes):
    slots = blocks.shape[0]
    chunk = 16
    sliver = COLS // planes
    return pl.pallas_call(
        functools.partial(cut_kernel, planes, chunk),
        grid=(slots // chunk,),
        in_specs=[SMEM, SMEM, pl.BlockSpec((chunk, 2, BPHI, COLS), lambda i: (i, 0, 0, 0))],
        out_specs=[pl.BlockSpec((chunk, sliver, LANES), lambda i: (i, 0, 0))] * planes,
        out_shape=[pltpu.HBM((slots, sliver, LANES), jnp.bfloat16)] * planes,
        compiler_params=params(),
        cost_estimate=LIGHT,
        name="cut",
    )(me, weight, *in_hbm(blocks))


def post_kernel(fields, tiles, capacity, slot_ref, note_ref, x_ref, out_ref, box_ref, buf, sems, out_sems):
    slots = slot_ref.shape[0]
    count = len(fields)
    rows = count * BPHI
    parts = sems.shape[0]
    some = slots // parts
    for k in range(parts):
        span = pl.ds(k * some, some)
        source = x_ref.at[span, pl.ds(fields[0], count)]
        pltpu.make_async_copy(source, buf.at[span], sems.at[k]).start()
    for t in range(tiles):
        box_ref[t, pl.ds(capacity * rows, NOTE)] = note_ref[...]
    for k in range(parts):
        span = pl.ds(k * some, some)
        pltpu.make_async_copy(buf.at[span], buf.at[span], sems.at[k]).wait()

        def body(i, carry):
            to = slot_ref[i]
            row = pl.multiple_of((to % capacity) * rows, rows)
            box_ref[to // capacity, pl.ds(row, rows)] = buf[i].reshape(rows, COLS)
            return carry

        lax.fori_loop(k * some, (k + 1) * some, body, 0)
    for t in range(tiles):
        pltpu.make_async_copy(box_ref.at[t], out_ref.at[t], out_sems.at[t]).start()
    for t in range(tiles):
        pltpu.make_async_copy(box_ref.at[t], out_ref.at[t], out_sems.at[t]).wait()


def post(blocks, slot, note, fields, tiles, capacity):
    slots = blocks.shape[0]
    rows = capacity * len(fields) * BPHI + NOTE
    return pl.pallas_call(
        functools.partial(post_kernel, fields, tiles, capacity),
        in_specs=[SMEM, VMEM, ANY],
        out_specs=HBM,
        out_shape=pltpu.HBM((tiles, rows, COLS), jnp.bfloat16),
        scratch_shapes=[
            pltpu.VMEM((tiles, rows, COLS), jnp.bfloat16),
            pltpu.VMEM((slots, len(fields), BPHI, COLS), jnp.bfloat16),
            pltpu.SemaphoreType.DMA((4,)),
            pltpu.SemaphoreType.DMA((tiles,)),
        ],
        compiler_params=params(),
        cost_estimate=LIGHT,
        name="post",
    )(slot, note, *in_hbm(blocks))


def sort_kernel(planes, count, capacity, me_ref, slot_ref, weight_ref, x_ref, *rest):
    outs, (buf, made, sems, out_sems) = rest[:-4], rest[-4:]
    tiles = buf.shape[0]
    per_plane = slot_ref.shape[0] // CG_DEV
    sliver = COLS // planes
    rows = count * BPHI
    me = me_ref[0]
    for t in range(tiles):
        pltpu.make_async_copy(x_ref.at[t], buf.at[t], sems.at[t]).start()
    for t in range(tiles):
        pltpu.make_async_copy(buf.at[t], buf.at[t], sems.at[t]).wait()

    def block(place, f):
        at = slot_ref[place]
        row = pl.multiple_of((at % capacity) * rows + f * BPHI, BPHI)
        return scaled(buf[at // capacity, pl.ds(row, BPHI)], weight_ref[place])

    for f in range(count):
        for j in range(per_plane // 2):

            def body(g, carry):
                even = block(2 * j * CG_DEV + g, f)
                odd = block((2 * j + 1) * CG_DEV + g, f)
                x = jnp.concatenate([even, odd], axis=0).T
                to = pl.ds(pl.multiple_of(g * sliver, sliver), sliver)
                for p in range(planes):
                    distance = (p - me + planes) % planes
                    made[f, distance, to, pl.ds(j * LANES, LANES)] = x[
                        p * sliver : (p + 1) * sliver
                    ]
                return carry

            lax.fori_loop(0, CG_DEV, body, 0, unroll=4)
        for d in range(planes):
            n = f * planes + d
            pltpu.make_async_copy(made.at[f, d], outs[d].at[f], out_sems.at[n]).start()
    for f in range(count):
        for d in range(planes):
            n = f * planes + d
            pltpu.make_async_copy(made.at[f, d], outs[d].at[f], out_sems.at[n]).wait()


def sort(arrived, slot, weight, me, planes, count, capacity):
    cells = slot.shape[0] // CG_DEV * BPHI
    slab = (CG_DEV * (COLS // planes), cells)
    return pl.pallas_call(
        functools.partial(sort_kernel, planes, count, capacity),
        in_specs=[SMEM, SMEM, SMEM, ANY],
        out_specs=[HBM] * planes,
        out_shape=[pltpu.HBM((count,) + slab, jnp.bfloat16)] * planes,
        scratch_shapes=[
            pltpu.VMEM(arrived.shape, jnp.bfloat16),
            pltpu.VMEM((count, planes) + slab, jnp.bfloat16),
            pltpu.SemaphoreType.DMA((arrived.shape[0],)),
            pltpu.SemaphoreType.DMA((count * planes,)),
        ],
        compiler_params=params(),
        cost_estimate=LIGHT,
        name="sort",
    )(me, slot, weight, *in_hbm(arrived))


def mail_kernel(planes, tiles, capacity, slot_ref, *rest):
    ins, (out_ref, box_ref, buf, sems, out_sems) = rest[:planes], rest[planes:]
    slots, sliver, _ = ins[0].shape
    for d in range(planes):
        pltpu.make_async_copy(ins[d], buf.at[d], sems.at[d]).start()
    for d in range(planes):
        pltpu.make_async_copy(buf.at[d], buf.at[d], sems.at[d]).wait()

        def body(i, carry):
            to = slot_ref[d, i]
            row = pl.multiple_of((to % (planes * capacity)) * sliver, sliver)
            box_ref[to // (planes * capacity), pl.ds(row, sliver)] = buf[d, i]
            return carry

        lax.fori_loop(0, slots, body, 0, unroll=4)
    for t in range(tiles):
        pltpu.make_async_copy(box_ref.at[t], out_ref.at[t], out_sems.at[t]).start()
    for t in range(tiles):
        pltpu.make_async_copy(box_ref.at[t], out_ref.at[t], out_sems.at[t]).wait()


def mail(parts, slot, tiles, capacity):
    planes = len(parts)
    slots, sliver, _ = parts[0].shape
    rows = planes * capacity * sliver
    return pl.pallas_call(
        functools.partial(mail_kernel, planes, tiles, capacity),
        in_specs=[SMEM] + [ANY] * planes,
        out_specs=HBM,
        out_shape=pltpu.HBM((tiles, rows, LANES), jnp.bfloat16),
        scratch_shapes=[
            pltpu.VMEM((tiles, rows, LANES), jnp.bfloat16),
            pltpu.VMEM((planes, slots, sliver, LANES), jnp.bfloat16),
            pltpu.SemaphoreType.DMA((planes,)),
            pltpu.SemaphoreType.DMA((tiles,)),
        ],
        compiler_params=params(),
        cost_estimate=LIGHT,
        name="mail",
    )(slot, *in_hbm(*parts))


def load_basis(basis_hbm, basis, sems):
    for j in range(SPANS):
        pltpu.make_async_copy(basis_hbm.at[j], basis.at[j], sems.at[j]).start()


def multiply(fields, base, basis, out_hbm, rows, acc, basis_sems, sems, steps=0, beside=None):
    wide = acc.shape[-1]
    copies = []
    for f in range(fields):
        for j in range(SPANS):
            n = len(copies)
            if f == 0:
                pltpu.make_async_copy(basis.at[j], basis.at[j], basis_sems.at[j]).wait()
                for step in range(j * steps // SPANS, (j + 1) * steps // SPANS):
                    beside(step)
            if n >= 2:
                copies[n - 2].wait()
            acc[n % 2] = jnp.dot(
                rows[f], basis[j], preferred_element_type=jnp.float32
            ).reshape(acc.shape[1:])
            copy = pltpu.make_async_copy(
                acc.at[n % 2], out_hbm.at[base + f, :, :, pl.ds(j * wide, wide)], sems.at[n % 2]
            )
            copy.start()
            copies.append(copy)
    for copy in copies[-2:]:
        copy.wait()


def rows_kernel(planes, take, base, chained, *refs):
    ins, basis_hbm = refs[:planes], refs[planes]
    out_hbm, rows, basis, acc, basis_sems, out_sems, in_sems = refs[planes + 1 + chained :]
    cells = ins[0].shape[2]
    for d in range(planes):
        to = rows.at[0, :, pl.ds(d * cells, cells)]
        pltpu.make_async_copy(ins[d].at[take], to, in_sems.at[d]).start()
    load_basis(basis_hbm, basis, basis_sems)
    for d in range(planes):
        to = rows.at[0, :, pl.ds(d * cells, cells)]
        pltpu.make_async_copy(to, to, in_sems.at[d]).wait()
    multiply(1, base, basis, out_hbm, rows, acc, basis_sems, out_sems)


def box_kernel(planes, per_plane, capacity, base, chained, *refs):
    slot_ref, box_hbm, basis_hbm = refs[:3]
    out_hbm, rows, basis, acc, basis_sems, out_sems, box, in_sems = refs[3 + chained :]
    tiles = box.shape[0]
    sliver = COLS // planes
    for t in range(tiles):
        pltpu.make_async_copy(box_hbm.at[t], box.at[t], in_sems.at[t]).start()
    load_basis(basis_hbm, basis, basis_sems)
    for t in range(tiles):
        pltpu.make_async_copy(box.at[t], box.at[t], in_sems.at[t]).wait()

    def piece(d, place):
        at = slot_ref[d, place]
        row = pl.multiple_of((at % (planes * capacity)) * sliver, sliver)
        return box[at // (planes * capacity), pl.ds(row, sliver)]

    def gather(field, d):
        cells = slice(0, BPHI) if field == 0 else slice(BPHI, LANES)
        for j in range(per_plane // 2):
            lanes = pl.ds((d * per_plane + 2 * j) * BPHI, LANES)
            for g in range(CG_DEV):
                even = piece(d, 2 * j * CG_DEV + g)
                odd = piece(d, (2 * j + 1) * CG_DEV + g)
                both = jnp.concatenate([even[:, cells], odd[:, cells]], axis=1)
                rows[field, pl.ds(g * sliver, sliver), lanes] = both

    for d in range(planes):
        gather(0, d)
    multiply(
        2, base, basis, out_hbm, rows, acc, basis_sems, out_sems, planes, lambda d: gather(1, d)
    )


def transform(kernel, operands, specs, total, basis, fields, planes, scratch, name):
    sliver = COLS // planes
    operands = operands + in_hbm(basis)
    specs = specs + [ANY]
    aliases = {}
    if total is not None:
        aliases = {len(operands): 0}
        operands, specs = operands + [total], specs + [ANY]
    return pl.pallas_call(
        kernel,
        in_specs=specs,
        out_specs=HBM,
        out_shape=pltpu.HBM((FIELDS, CG_DEV, sliver, NPHI), jnp.float32),
        scratch_shapes=[
            pltpu.VMEM((fields, CG_DEV * sliver, NPHI), jnp.bfloat16),
            pltpu.VMEM((SPANS, NPHI, NPHI // SPANS), jnp.bfloat16),
            pltpu.VMEM((2, CG_DEV, sliver, NPHI // SPANS), jnp.float32),
            pltpu.SemaphoreType.DMA((SPANS,)),
            pltpu.SemaphoreType.DMA((2,)),
        ]
        + scratch,
        input_output_aliases=aliases,
        compiler_params=params(),
        cost_estimate=LIGHT,
        name=name,
    )(*operands)


def transform_rows(slabs, take, basis, total, base):
    planes = len(slabs)
    kernel = functools.partial(rows_kernel, planes, take, base, int(total is not None))
    scratch = [pltpu.SemaphoreType.DMA((planes,))]
    return transform(
        kernel, in_hbm(*slabs), [ANY] * planes, total, basis, 1, planes, scratch, "rows"
    )


def transform_box(box, slot, basis, total, base, per_plane, capacity):
    planes = slot.shape[0]
    kernel = functools.partial(box_kernel, planes, per_plane, capacity, base, int(total is not None))
    scratch = [pltpu.VMEM(box.shape, jnp.bfloat16), pltpu.SemaphoreType.DMA((box.shape[0],))]
    return transform(kernel, [slot] + in_hbm(box), [SMEM, ANY], total, basis, 2, planes, scratch, "box")


def rank_of(dest):
    slots = dest.shape[-1]
    at = jnp.arange(slots, dtype=jnp.int32)
    same = (dest[..., :, None] == dest[..., None, :]) & (at[None, :] < at[:, None])
    return jnp.sum(same.astype(jnp.int32), axis=-1)


def as_note(dest, place_level, width):
    count = dest.size
    pad = -count % width
    each = (count + pad) // width
    codes = [jnp.pad(c.reshape(-1), (0, pad)).reshape(each, width) for c in (dest, place_level)]
    both = jnp.concatenate(codes, axis=0)
    return jnp.pad(both, ((0, NOTE - 2 * each), (0, 0))).astype(jnp.bfloat16)


def from_note(box, count):
    width = box.shape[2]
    each = -(-count // width)
    note = box[:, box.shape[1] - NOTE :, :].astype(jnp.float32).astype(jnp.int32)
    dest = note[:, :each].reshape(-1, each * width)[:, :count]
    place_level = note[:, each : 2 * each].reshape(-1, each * width)[:, :count]
    return dest, place_level


def local(blocks, levels, block_dest, block_phi, block_group):
    tiles = lax.axis_size("tile")
    planes = lax.axis_size("phi")
    tile = lax.axis_index("tile")
    plane = lax.axis_index("phi")
    slots = blocks.shape[0]
    per_plane = NPHI // BPHI // planes
    places = per_plane * CG_DEV
    capacity = 2 * slots // tiles
    me = plane.astype(jnp.int32).reshape(1)
    weight = 1.0 / jnp.left_shift(1, levels).astype(jnp.float32)
    place_iota = jnp.arange(places, dtype=jnp.int32)

    def over_phi(parts):
        moved = [parts[0]]
        for d in range(1, planes):
            pairs = [(s, (s + d) % planes) for s in range(planes)]
            moved.append(lax.ppermute(parts[d], "phi", pairs))
        return moved

    def over_tile(box):
        return lax.all_to_all(box, "tile", split_axis=0, concat_axis=0, tiled=True)

    def tie(value, *others):
        return lax.optimization_barrier((value,) + others)[0]

    place_level = levels * places + block_phi * CG_DEV + block_group
    own_slot = block_dest * capacity + rank_of(block_dest)
    own_note = as_note(block_dest, place_level, COLS)
    box = post(blocks, own_slot, own_note, GROUPS[0], tiles, capacity)
    pieces = cut(blocks, weight, me, planes)

    back = (plane - jnp.arange(planes, dtype=jnp.int32)) % planes
    basis = rotated_basis(NPHI, back)

    code = tie(block_dest * (4 * places) + place_level, pieces[0])
    codes = jnp.stack(over_phi([code] * planes))
    dest = codes // (4 * places)
    distance = jnp.arange(planes, dtype=jnp.int32)[:, None]
    out_slot = (dest * planes + distance) * capacity + rank_of(dest)
    out_note = as_note(dest, codes % (4 * places), COLS)
    next_box = post(blocks, own_slot, out_note, GROUPS[1], tiles, capacity)

    first = over_tile(box)
    sent = over_phi(pieces)
    second = over_tile(tie(next_box, first, basis, *sent))

    got_dest, got_code = from_note(first, slots)
    got_slot = jnp.arange(tiles, dtype=jnp.int32)[:, None] * capacity + rank_of(got_dest)
    here = (got_dest == tile)[..., None] & ((got_code % places)[..., None] == place_iota)
    slot = jnp.sum(jnp.where(here, got_slot[..., None], 0), axis=(0, 1))
    level = jnp.sum(jnp.where(here, (got_code // places)[..., None], 0), axis=(0, 1))
    got_weight = 1.0 / jnp.left_shift(1, level).astype(jnp.float32)

    outbox = mail(sent, out_slot, tiles, capacity)
    early = over_phi(sort(first, slot, got_weight, me, planes, 2, capacity))
    last = over_tile(tie(outbox, second, early[1], early[planes - 1]))
    rest = sort(second, slot, got_weight, me, planes, 1, capacity)
    rest = list(lax.optimization_barrier((tuple(rest), tuple(early)))[0])

    from_dest, from_code = from_note(second, planes * slots)
    from_dest = from_dest.reshape(tiles, planes, slots)
    from_place = from_code.reshape(tiles, planes, slots) % places
    start = jnp.arange(tiles, dtype=jnp.int32)[:, None, None] * planes + distance
    from_slot = start * capacity + rank_of(from_dest)
    here = (from_dest == tile)[..., None] & (from_place[..., None] == place_iota)
    routed = jnp.sum(jnp.where(here, from_slot[..., None], 0), axis=(0, 2))

    early = [tie(early[0], *rest)] + early[1:]
    rest = over_phi(rest)
    total = transform_rows(early, 0, basis, None, GROUPS[0][0])
    total = transform_rows(early, 1, basis, total, GROUPS[0][1])
    total = transform_rows(rest, 0, basis, total, GROUPS[1][0])
    return transform_box(last, routed, basis, total, PAIR[0], per_plane, capacity)


def solution(mesh):
    in_specs = (
        P(("tile", "phi"), None, None, None),
        P(("tile", "phi")),
        P(("tile", "phi")),
        P(("tile", "phi")),
        P(("tile", "phi")),
    )
    out_specs = P(None, "tile", "phi", None)
    return jax.shard_map(local, mesh=mesh, in_specs=in_specs, out_specs=out_specs, check_vma=False)
```

```python
import functools
import math

import jax
import jax.numpy as jnp
from jax import lax
from jax.experimental import pallas as pl
from jax.experimental.pallas import tpu as pltpu
from jax.sharding import PartitionSpec as P

FIELDS = 5
NPHI = 2048
BPHI = 64
COLS = 256
CG_DEV = 8
LANES = 128
NOTE = 16
PAIR = (0, 1)
GROUPS = ((2, 3), (4,))
VMEM_BYTES = 32 * 1024 * 1024
SPANS = 4
LIGHT = pl.CostEstimate(flops=0, bytes_accessed=0, transcendentals=0)
SLOW = pl.CostEstimate(flops=20_000_000_000, bytes_accessed=0, transcendentals=0)
SLOWER = pl.CostEstimate(flops=30_000_000_000, bytes_accessed=0, transcendentals=0)

ANY = pl.BlockSpec(memory_space=pl.ANY)
HBM = pl.BlockSpec(memory_space=pltpu.HBM)
SMEM = pl.BlockSpec(memory_space=pltpu.SMEM)
VMEM = pl.BlockSpec(memory_space=pltpu.VMEM)


def rotated_basis(length, back):
    planes = back.shape[0]
    per = length // planes
    column = jnp.arange(length, dtype=jnp.int32)
    half = length // 2
    mode = jnp.where(column <= half, column, column - half)
    coarse = (back[:, None] * per + jnp.arange(0, per, BPHI, dtype=jnp.int32)[None, :]).reshape(-1)
    fine = jnp.arange(BPHI, dtype=jnp.int32)

    def angle(row):
        phase = row[:, None] * mode[None, :] % length
        return phase.astype(jnp.float32) * jnp.float32(2.0 * math.pi / length)

    even = (column <= half)[None, :]
    scale = jnp.float32(1.0 / math.sqrt(length))
    far, near = angle(coarse), angle(fine)
    by_cos = jnp.where(even, jnp.cos(far), jnp.sin(far)) * scale
    by_sin = jnp.where(even, -jnp.sin(far), jnp.cos(far)) * scale
    near_cos, near_sin = jnp.cos(near), jnp.sin(near)

    def spans(x):
        return x.reshape(x.shape[0], SPANS, length // SPANS).transpose(1, 0, 2)

    by_cos, by_sin = spans(by_cos)[:, :, None], spans(by_sin)[:, :, None]
    near_cos, near_sin = spans(near_cos)[:, None], spans(near_sin)[:, None]
    by_cos, by_sin, near_cos, near_sin = lax.optimization_barrier((by_cos, by_sin, near_cos, near_sin))
    table = by_cos * near_cos + by_sin * near_sin
    return table.reshape(SPANS, length, length // SPANS).astype(jnp.bfloat16)


def in_hbm(*arrays):
    return [pltpu.with_memory_space_constraint(a, pltpu.HBM) for a in arrays]


def params():
    return pltpu.CompilerParams(vmem_limit_bytes=VMEM_BYTES)


def scaled(block, weight):
    return block * jnp.full((1, 1), weight, jnp.float32).astype(jnp.bfloat16)


def cut_kernel(planes, me_ref, weight_ref, note_ref, x_ref, *refs):
    outs, (buf, made, sems, out_sems) = refs[:planes], refs[planes:]
    slots = buf.shape[0]
    sliver = COLS // planes
    parts = sems.shape[0]
    some = slots // parts
    me = me_ref[0]
    for k in range(parts):
        span = pl.ds(k * some, some)
        source = x_ref.at[span, pl.ds(PAIR[0], 2)]
        pltpu.make_async_copy(source, buf.at[span], sems.at[k]).start()
    for d in range(planes):
        made[d, pl.ds(slots * sliver, NOTE)] = note_ref[...]

    def leave(k, d):
        rows = some * sliver + (NOTE if k == parts - 1 else 0)
        span = pl.ds(k * some * sliver, rows)
        return pltpu.make_async_copy(made.at[d, span], outs[d].at[span], out_sems.at[k, d])

    for k in range(parts):
        span = pl.ds(k * some, some)
        pltpu.make_async_copy(buf.at[span], buf.at[span], sems.at[k]).wait()

        def body(i, carry):
            x = scaled(buf[i].reshape(LANES, COLS), weight_ref[i]).T
            to = pl.ds(pl.multiple_of(i * sliver, sliver), sliver)
            for p in range(planes):
                made[(p - me + planes) % planes, to] = x[p * sliver : (p + 1) * sliver]
            return carry

        lax.fori_loop(k * some, (k + 1) * some, body, 0, unroll=4)
        for d in range(planes):
            leave(k, d).start()
    for k in range(parts):
        for d in range(planes):
            leave(k, d).wait()


def cut(blocks, weight, note, me, planes):
    slots = blocks.shape[0]
    parts = 4
    rows = slots * (COLS // planes) + NOTE
    return pl.pallas_call(
        functools.partial(cut_kernel, planes),
        in_specs=[SMEM, SMEM, VMEM, ANY],
        out_specs=[HBM] * planes,
        out_shape=[pltpu.HBM((rows, LANES), jnp.bfloat16)] * planes,
        scratch_shapes=[
            pltpu.VMEM((slots, 2, BPHI, COLS), jnp.bfloat16),
            pltpu.VMEM((planes, rows, LANES), jnp.bfloat16),
            pltpu.SemaphoreType.DMA((parts,)),
            pltpu.SemaphoreType.DMA((parts, planes)),
        ],
        compiler_params=params(),
        cost_estimate=LIGHT,
        name="cut",
    )(me, weight, note, *in_hbm(blocks))


def post_kernel(
    fields, tiles, capacity, dest_ref, note_ref, x_ref, out_ref, box_ref, buf, filled, sems, out_sems
):
    slots = dest_ref.shape[0]
    count = len(fields)
    rows = count * BPHI
    parts = sems.shape[0]
    some = slots // parts
    for k in range(parts):
        span = pl.ds(k * some, some)
        source = x_ref.at[span, pl.ds(fields[0], count)]
        pltpu.make_async_copy(source, buf.at[span], sems.at[k]).start()
    for t in range(tiles):
        filled[t] = 0
        box_ref[t, pl.ds(capacity * rows, NOTE)] = note_ref[...]
    for k in range(parts):
        span = pl.ds(k * some, some)
        pltpu.make_async_copy(buf.at[span], buf.at[span], sems.at[k]).wait()

        def body(i, carry):
            tile = dest_ref[i]
            slot = filled[tile]
            filled[tile] = slot + 1
            row = pl.multiple_of(slot * rows, rows)
            box_ref[tile, pl.ds(row, rows)] = buf[i].reshape(rows, COLS)
            return carry

        lax.fori_loop(k * some, (k + 1) * some, body, 0)
    for t in range(tiles):
        pltpu.make_async_copy(box_ref.at[t], out_ref.at[t], out_sems.at[t]).start()
    for t in range(tiles):
        pltpu.make_async_copy(box_ref.at[t], out_ref.at[t], out_sems.at[t]).wait()


def post(blocks, dest, note, fields, tiles, capacity):
    slots = blocks.shape[0]
    rows = capacity * len(fields) * BPHI + NOTE
    return pl.pallas_call(
        functools.partial(post_kernel, fields, tiles, capacity),
        in_specs=[SMEM, VMEM, ANY],
        out_specs=HBM,
        out_shape=pltpu.HBM((tiles, rows, COLS), jnp.bfloat16),
        scratch_shapes=[
            pltpu.VMEM((tiles, rows, COLS), jnp.bfloat16),
            pltpu.VMEM((slots, len(fields), BPHI, COLS), jnp.bfloat16),
            pltpu.SMEM((tiles,), jnp.int32),
            pltpu.SemaphoreType.DMA((4,)),
            pltpu.SemaphoreType.DMA((tiles,)),
        ],
        compiler_params=params(),
        cost_estimate=LIGHT,
        name="post",
    )(dest, note, *in_hbm(blocks))


def sort_kernel(planes, count, capacity, me_ref, slot_ref, weight_ref, note_ref, x_ref, *rest):
    outs, (buf, made, sems, out_sems) = rest[:-4], rest[-4:]
    tiles = buf.shape[0]
    per_plane = slot_ref.shape[0] // CG_DEV
    sliver = COLS // planes
    rows = count * BPHI
    side = CG_DEV * sliver
    me = me_ref[0]
    for d in range(planes):
        made[d, pl.ds(count * side, NOTE)] = note_ref[...]
    for t in range(tiles):
        pltpu.make_async_copy(x_ref.at[t], buf.at[t], sems.at[t]).start()
    for t in range(tiles):
        pltpu.make_async_copy(buf.at[t], buf.at[t], sems.at[t]).wait()

    def leave(f, d):
        span = pl.ds(f * side, side + (NOTE if f == count - 1 else 0))
        return pltpu.make_async_copy(made.at[d, span], outs[d].at[span], out_sems.at[f, d])

    def block(place, f):
        at = slot_ref[place]
        row = pl.multiple_of((at % capacity) * rows + f * BPHI, BPHI)
        return scaled(buf[at // capacity, pl.ds(row, BPHI)], weight_ref[place])

    for f in range(count):
        for j in range(per_plane // 2):

            def body(g, carry):
                even = block(2 * j * CG_DEV + g, f)
                odd = block((2 * j + 1) * CG_DEV + g, f)
                x = jnp.concatenate([even, odd], axis=0).T
                to = pl.ds(pl.multiple_of(f * side + g * sliver, sliver), sliver)
                for p in range(planes):
                    distance = (p - me + planes) % planes
                    made[distance, to, pl.ds(j * LANES, LANES)] = x[p * sliver : (p + 1) * sliver]
                return carry

            lax.fori_loop(0, CG_DEV, body, 0, unroll=4)
        for d in range(planes):
            leave(f, d).start()
    for f in range(count):
        for d in range(planes):
            leave(f, d).wait()


def sort(arrived, slot, weight, note, me, planes, count, capacity):
    cells = slot.shape[0] // CG_DEV * BPHI
    rows = count * CG_DEV * (COLS // planes) + NOTE
    return pl.pallas_call(
        functools.partial(sort_kernel, planes, count, capacity),
        in_specs=[SMEM, SMEM, SMEM, VMEM, ANY],
        out_specs=[HBM] * planes,
        out_shape=[pltpu.HBM((rows, cells), jnp.bfloat16)] * planes,
        scratch_shapes=[
            pltpu.VMEM(arrived.shape, jnp.bfloat16),
            pltpu.VMEM((planes, rows, cells), jnp.bfloat16),
            pltpu.SemaphoreType.DMA((arrived.shape[0],)),
            pltpu.SemaphoreType.DMA((count, planes)),
        ],
        compiler_params=params(),
        cost_estimate=LIGHT,
        name="sort",
    )(me, slot, weight, note, *in_hbm(arrived))


def mail_kernel(planes, tiles, capacity, slot_ref, *refs):
    ins, (out_ref, box_ref, buf, sems, out_sems) = refs[:planes], refs[planes:]
    slots = slot_ref.shape[1]
    sliver = box_ref.shape[1] // (planes * capacity)
    for d in range(planes):
        source = ins[d].at[pl.ds(0, slots * sliver)]
        pltpu.make_async_copy(source, buf.at[d], sems.at[d]).start()
    for d in range(planes):
        pltpu.make_async_copy(buf.at[d], buf.at[d], sems.at[d]).wait()

        def body(i, carry):
            to = slot_ref[d, i]
            row = pl.multiple_of((to % (planes * capacity)) * sliver, sliver)
            source = pl.ds(pl.multiple_of(i * sliver, sliver), sliver)
            box_ref[to // (planes * capacity), pl.ds(row, sliver)] = buf[d, source]
            return carry

        lax.fori_loop(0, slots, body, 0, unroll=4)
    for t in range(tiles):
        pltpu.make_async_copy(box_ref.at[t], out_ref.at[t], out_sems.at[t]).start()
    for t in range(tiles):
        pltpu.make_async_copy(box_ref.at[t], out_ref.at[t], out_sems.at[t]).wait()


def mail(parts, slot, tiles, capacity):
    planes, slots = slot.shape
    sliver = COLS // planes
    rows = planes * capacity * sliver
    return pl.pallas_call(
        functools.partial(mail_kernel, planes, tiles, capacity),
        in_specs=[SMEM] + [ANY] * planes,
        out_specs=HBM,
        out_shape=pltpu.HBM((tiles, rows, LANES), jnp.bfloat16),
        scratch_shapes=[
            pltpu.VMEM((tiles, rows, LANES), jnp.bfloat16),
            pltpu.VMEM((planes, slots * sliver, LANES), jnp.bfloat16),
            pltpu.SemaphoreType.DMA((planes,)),
            pltpu.SemaphoreType.DMA((tiles,)),
        ],
        compiler_params=params(),
        cost_estimate=SLOW,
        name="mail",
    )(slot, *in_hbm(*parts))


def load_basis(basis_hbm, basis, sems, spans):
    for j in spans:
        pltpu.make_async_copy(basis_hbm.at[j], basis.at[j], sems.at[j]).start()


def multiply(order, basis, out_hbm, rows, acc, basis_sems, sems, beside=None):
    wide = acc.shape[-1]
    copies = []
    for f, field in enumerate(order):
        for j in range(SPANS):
            n = len(copies)
            if f == 0:
                pltpu.make_async_copy(basis.at[j], basis.at[j], basis_sems.at[j]).wait()
            if beside is not None:
                beside(n)
            if n >= 2:
                copies[n - 2].wait()
            acc[n % 2] = jnp.dot(
                rows[f][...], basis[j], preferred_element_type=jnp.float32
            ).reshape(acc.shape[1:])
            copy = pltpu.make_async_copy(
                acc.at[n % 2], out_hbm.at[field, :, :, pl.ds(j * wide, wide)], sems.at[n % 2]
            )
            copy.start()
            copies.append(copy)
    for copy in copies[-2:]:
        copy.wait()


def load_rows(ins, take, rows, sems):
    cells = ins[0].shape[1]
    side = rows.shape[0]
    for d in range(len(ins)):
        to = rows.at[:, pl.ds(d * cells, cells)]
        pltpu.make_async_copy(ins[d].at[pl.ds(take * side, side)], to, sems.at[d]).start()


def wait_rows(planes, rows, sems):
    cells = rows.shape[1] // planes
    for d in range(planes):
        to = rows.at[:, pl.ds(d * cells, cells)]
        pltpu.make_async_copy(to, to, sems.at[d]).wait()


def rows_kernel(planes, take, field, chained, *refs):
    ins, basis_hbm = refs[:planes], refs[planes]
    out_hbm, rows, basis, acc, in_sems, basis_sems, out_sems = refs[planes + 1 + chained :]
    load_rows(ins, take, rows, in_sems)
    load_basis(basis_hbm, basis, basis_sems, range(SPANS))
    wait_rows(planes, rows, in_sems)
    multiply((field,), basis, out_hbm, (rows,), acc, basis_sems, out_sems)


def last_kernel(planes, per_plane, capacity, order, *refs):
    slot_ref, ins, (box_hbm, basis_hbm, _, out_hbm) = refs[0], refs[1 : 1 + planes], refs[1 + planes : 5 + planes]
    rows, one, two, basis, acc, box, in_sems, box_sems, basis_sems, out_sems = refs[5 + planes :]
    tiles = box.shape[0]
    sliver = COLS // planes
    load_rows(ins, 0, rows, in_sems)
    load_basis(basis_hbm, basis, basis_sems, range(1))
    for t in range(tiles):
        pltpu.make_async_copy(box_hbm.at[t], box.at[t], box_sems.at[t]).start()
    load_basis(basis_hbm, basis, basis_sems, range(1, SPANS))

    def piece(d, place):
        at = slot_ref[d, place]
        row = pl.multiple_of((at % (planes * capacity)) * sliver, sliver)
        return box[at // (planes * capacity), pl.ds(row, sliver)]

    def gather(rows, cells, d):
        for j in range(per_plane // 2):
            lanes = pl.ds((d * per_plane + 2 * j) * BPHI, LANES)
            for g in range(CG_DEV):
                even = piece(d, 2 * j * CG_DEV + g)
                odd = piece(d, (2 * j + 1) * CG_DEV + g)
                both = jnp.concatenate([even[:, cells], odd[:, cells]], axis=1)
                rows[pl.ds(g * sliver, sliver), lanes] = both

    def beside(n):
        if n == 1:
            for t in range(tiles):
                pltpu.make_async_copy(box.at[t], box.at[t], box_sems.at[t]).wait()
        first = SPANS - 1
        for d in range(planes):
            if n == 1 + d * first // planes:
                gather(one, slice(0, BPHI), d)
            if n == SPANS + d * SPANS // planes:
                gather(two, slice(BPHI, LANES), d)

    wait_rows(planes, rows, in_sems)
    multiply(order, basis, out_hbm, (rows, one, two), acc, basis_sems, out_sems, beside)


def transform(kernel, operands, specs, total, basis, planes, extra, name):
    sliver = COLS // planes
    operands = operands + in_hbm(basis)
    specs = specs + [ANY]
    aliases = {}
    if total is not None:
        aliases = {len(operands): 0}
        operands, specs = operands + [total], specs + [ANY]
    rows = pltpu.VMEM((CG_DEV * sliver, NPHI), jnp.bfloat16)
    more, sems = extra
    return pl.pallas_call(
        kernel,
        in_specs=specs,
        out_specs=HBM,
        out_shape=pltpu.HBM((FIELDS, CG_DEV, sliver, NPHI), jnp.float32),
        scratch_shapes=[rows] * (3 if more else 1)
        + [
            pltpu.VMEM((SPANS, NPHI, NPHI // SPANS), jnp.bfloat16),
            pltpu.VMEM((2, CG_DEV, sliver, NPHI // SPANS), jnp.float32),
        ]
        + more
        + [pltpu.SemaphoreType.DMA((planes,))]
        + sems
        + [pltpu.SemaphoreType.DMA((SPANS,)), pltpu.SemaphoreType.DMA((2,))],
        input_output_aliases=aliases,
        compiler_params=params(),
        cost_estimate=SLOWER if name == "rows" else LIGHT,
        name=name,
    )(*operands)


def transform_rows(slabs, take, basis, total, field):
    planes = len(slabs)
    kernel = functools.partial(rows_kernel, planes, take, field, int(total is not None))
    return transform(kernel, in_hbm(*slabs), [ANY] * planes, total, basis, planes, ([], []), "rows")


def transform_last(slabs, box, slot, basis, total, order, per_plane, capacity):
    planes = slot.shape[0]
    kernel = functools.partial(last_kernel, planes, per_plane, capacity, order)
    extra = ([pltpu.VMEM(box.shape, jnp.bfloat16)], [pltpu.SemaphoreType.DMA((box.shape[0],))])
    operands, specs = [slot] + in_hbm(*slabs, box), [SMEM] + [ANY] * (planes + 1)
    return transform(kernel, operands, specs, total, basis, planes, extra, "last")


def rank_of(dest):
    slots = dest.shape[-1]
    at = jnp.arange(slots, dtype=jnp.int32)
    same = (dest[..., :, None] == dest[..., None, :]) & (at[None, :] < at[:, None])
    return jnp.sum(same.astype(jnp.int32), axis=-1)


def as_note(dest, place_level, width):
    count = dest.size
    pad = -count % width
    each = (count + pad) // width
    codes = [jnp.pad(c.reshape(-1), (0, pad)).reshape(each, width) for c in (dest, place_level)]
    both = jnp.concatenate(codes, axis=0)
    return jnp.pad(both, ((0, NOTE - 2 * each), (0, 0))).astype(jnp.bfloat16)


def from_note(note, count):
    width = note.shape[2]
    each = -(-count // width)
    note = note.astype(jnp.float32).astype(jnp.int32)
    dest = note[:, :each].reshape(-1, each * width)[:, :count]
    place_level = note[:, each : 2 * each].reshape(-1, each * width)[:, :count]
    return dest, place_level


def local(blocks, levels, block_dest, block_phi, block_group):
    tiles = lax.axis_size("tile")
    planes = lax.axis_size("phi")
    tile = lax.axis_index("tile")
    plane = lax.axis_index("phi")
    slots = blocks.shape[0]
    per_plane = NPHI // BPHI // planes
    places = per_plane * CG_DEV
    capacity = 2 * slots // tiles
    me = plane.astype(jnp.int32).reshape(1)
    weight = 1.0 / jnp.left_shift(1, levels).astype(jnp.float32)
    place_iota = jnp.arange(places, dtype=jnp.int32)

    def over_phi(parts):
        moved = [parts[0]]
        for d in range(1, planes):
            pairs = [(s, (s + d) % planes) for s in range(planes)]
            moved.append(lax.ppermute(parts[d], "phi", pairs))
        return moved

    def over_tile(box):
        return lax.all_to_all(box, "tile", split_axis=0, concat_axis=0, tiled=True)

    def tie(value, *others):
        return lax.optimization_barrier((value,) + others)[0]

    place_level = levels * places + block_phi * CG_DEV + block_group
    distance = jnp.arange(planes, dtype=jnp.int32)[:, None]
    box_note = as_note(block_dest, place_level, COLS)
    box = post(blocks, block_dest, box_note, GROUPS[0], tiles, capacity)
    pieces = cut(blocks, weight, as_note(block_dest, place_level, LANES), me, planes)
    next_box = post(tie(blocks, pieces[0]), block_dest, box_note, GROUPS[1], tiles, capacity)

    back = (plane - jnp.arange(planes, dtype=jnp.int32)) % planes
    basis = rotated_basis(NPHI, back)

    first = over_tile(box)
    sent = over_phi(pieces)
    second = over_tile(tie(next_box, first, basis, sent[1], sent[planes - 1]))

    got_dest, got_code = from_note(first[:, -NOTE:], slots)
    got_slot = jnp.arange(tiles, dtype=jnp.int32)[:, None] * capacity + rank_of(got_dest)
    here = (got_dest == tile)[..., None] & ((got_code % places)[..., None] == place_iota)
    slot = jnp.sum(jnp.where(here, got_slot[..., None], 0), axis=(0, 1))
    level = jnp.sum(jnp.where(here, (got_code // places)[..., None], 0), axis=(0, 1))
    got_weight = 1.0 / jnp.left_shift(1, level).astype(jnp.float32)
    note = as_note(got_dest, got_code, per_plane * BPHI)

    dest, _ = from_note(jnp.stack([part[-NOTE:] for part in sent]), slots)
    out_slot = (dest * planes + distance) * capacity + rank_of(dest)

    arrived = tie(first, *sent[1:])
    early = over_phi(sort(arrived, slot, got_weight, note, me, planes, 2, capacity))
    outbox = mail(sent, out_slot, tiles, capacity)
    last = over_tile(tie(outbox, second))
    rest = sort(second, slot, got_weight, note, me, planes, 1, capacity)
    early = [tie(early[0], *rest)] + early[1:]
    rest = over_phi(rest)

    from_dest, from_code = from_note(jnp.stack([part[-NOTE:] for part in early]), tiles * slots)
    from_dest = from_dest.reshape(planes, tiles, slots)
    from_place = from_code.reshape(planes, tiles, slots) % places
    start = jnp.arange(tiles, dtype=jnp.int32)[None, :, None] * planes + distance[..., None]
    from_slot = start * capacity + rank_of(from_dest)
    here = (from_dest == tile)[..., None] & (from_place[..., None] == place_iota)
    routed = jnp.sum(jnp.where(here, from_slot[..., None], 0), axis=(1, 2))

    total = transform_rows(early, 0, basis, None, GROUPS[0][0])
    total = transform_rows(early, 1, basis, total, GROUPS[0][1])
    order = GROUPS[1] + PAIR
    return transform_last(rest, last, routed, basis, total, order, per_plane, capacity)


def solution(mesh):
    in_specs = (
        P(("tile", "phi"), None, None, None),
        P(("tile", "phi")),
        P(("tile", "phi")),
        P(("tile", "phi")),
        P(("tile", "phi")),
    )
    out_specs = P(None, "tile", "phi", None)
    return jax.shard_map(local, mesh=mesh, in_specs=in_specs, out_specs=out_specs, check_vma=False)
```

```python
import functools
import math

import jax
import jax.numpy as jnp
from jax import lax
from jax.experimental import pallas as pl
from jax.experimental.pallas import tpu as pltpu
from jax.sharding import PartitionSpec as P

FIELDS = 5
NPHI = 2048
BPHI = 64
COLS = 256
CG_DEV = 8
LANES = 128
NOTE = 16
PAIR = (0, 1)
GROUPS = ((2, 3), (4,))
VMEM_BYTES = 32 * 1024 * 1024
SPANS = 4
LIGHT = pl.CostEstimate(flops=0, bytes_accessed=0, transcendentals=0)
SLOW = pl.CostEstimate(flops=20_000_000_000, bytes_accessed=0, transcendentals=0)
SLOWER = pl.CostEstimate(flops=30_000_000_000, bytes_accessed=0, transcendentals=0)

ANY = pl.BlockSpec(memory_space=pl.ANY)
HBM = pl.BlockSpec(memory_space=pltpu.HBM)
SMEM = pl.BlockSpec(memory_space=pltpu.SMEM)
VMEM = pl.BlockSpec(memory_space=pltpu.VMEM)


def rotated_basis(length, back):
    planes = back.shape[0]
    per = length // planes
    column = jnp.arange(length, dtype=jnp.int32)
    half = length // 2
    mode = jnp.where(column <= half, column, column - half)
    coarse = (back[:, None] * per + jnp.arange(0, per, BPHI, dtype=jnp.int32)[None, :]).reshape(-1)
    fine = jnp.arange(BPHI, dtype=jnp.int32)

    def angle(row):
        phase = row[:, None] * mode[None, :] % length
        return phase.astype(jnp.float32) * jnp.float32(2.0 * math.pi / length)

    even = (column <= half)[None, :]
    scale = jnp.float32(1.0 / math.sqrt(length))
    far, near = angle(coarse), angle(fine)
    by_cos = jnp.where(even, jnp.cos(far), jnp.sin(far)) * scale
    by_sin = jnp.where(even, -jnp.sin(far), jnp.cos(far)) * scale
    near_cos, near_sin = jnp.cos(near), jnp.sin(near)

    def spans(x):
        return x.reshape(x.shape[0], SPANS, length // SPANS).transpose(1, 0, 2)

    by_cos, by_sin = spans(by_cos)[:, :, None], spans(by_sin)[:, :, None]
    near_cos, near_sin = spans(near_cos)[:, None], spans(near_sin)[:, None]
    by_cos, by_sin, near_cos, near_sin = lax.optimization_barrier((by_cos, by_sin, near_cos, near_sin))
    table = by_cos * near_cos + by_sin * near_sin
    return table.reshape(SPANS, length, length // SPANS).astype(jnp.bfloat16)


def in_hbm(*arrays):
    return [pltpu.with_memory_space_constraint(a, pltpu.HBM) for a in arrays]


def params():
    return pltpu.CompilerParams(vmem_limit_bytes=VMEM_BYTES)


def scaled(block, weight):
    return block * jnp.full((1, 1), weight, jnp.float32).astype(jnp.bfloat16)


def cut_kernel(planes, me_ref, weight_ref, note_ref, x_ref, *refs):
    outs, (buf, made, sems, out_sems) = refs[:planes], refs[planes:]
    slots = buf.shape[0]
    sliver = COLS // planes
    parts = sems.shape[0]
    some = slots // parts
    me = me_ref[0]
    for k in range(parts):
        span = pl.ds(k * some, some)
        source = x_ref.at[span, pl.ds(PAIR[0], 2)]
        pltpu.make_async_copy(source, buf.at[span], sems.at[k]).start()
    for d in range(planes):
        made[d, pl.ds(slots * sliver, NOTE)] = note_ref[...]

    def leave(k, d):
        rows = some * sliver + (NOTE if k == parts - 1 else 0)
        span = pl.ds(k * some * sliver, rows)
        return pltpu.make_async_copy(made.at[d, span], outs[d].at[span], out_sems.at[k, d])

    for k in range(parts):
        span = pl.ds(k * some, some)
        pltpu.make_async_copy(buf.at[span], buf.at[span], sems.at[k]).wait()

        def body(i, carry):
            x = scaled(buf[i].reshape(LANES, COLS), weight_ref[i]).T
            to = pl.ds(pl.multiple_of(i * sliver, sliver), sliver)
            for p in range(planes):
                made[(p - me + planes) % planes, to] = x[p * sliver : (p + 1) * sliver]
            return carry

        lax.fori_loop(k * some, (k + 1) * some, body, 0, unroll=4)
        for d in range(planes):
            leave(k, d).start()
    for k in range(parts):
        for d in range(planes):
            leave(k, d).wait()


def cut(blocks, weight, note, me, planes):
    slots = blocks.shape[0]
    parts = 4
    rows = slots * (COLS // planes) + NOTE
    return pl.pallas_call(
        functools.partial(cut_kernel, planes),
        in_specs=[SMEM, SMEM, VMEM, ANY],
        out_specs=[HBM] * planes,
        out_shape=[pltpu.HBM((rows, LANES), jnp.bfloat16)] * planes,
        scratch_shapes=[
            pltpu.VMEM((slots, 2, BPHI, COLS), jnp.bfloat16),
            pltpu.VMEM((planes, rows, LANES), jnp.bfloat16),
            pltpu.SemaphoreType.DMA((parts,)),
            pltpu.SemaphoreType.DMA((parts, planes)),
        ],
        compiler_params=params(),
        cost_estimate=LIGHT,
        name="cut",
    )(me, weight, note, *in_hbm(blocks))


def post_kernel(
    fields, tiles, capacity, dest_ref, note_ref, x_ref, out_ref, box_ref, buf, filled, sems, out_sems
):
    slots = dest_ref.shape[0]
    count = len(fields)
    rows = count * BPHI
    parts = sems.shape[0]
    some = slots // parts
    for k in range(parts):
        span = pl.ds(k * some, some)
        source = x_ref.at[span, pl.ds(fields[0], count)]
        pltpu.make_async_copy(source, buf.at[span], sems.at[k]).start()
    for t in range(tiles):
        filled[t] = 0
        box_ref[t, pl.ds(capacity * rows, NOTE)] = note_ref[...]
    for k in range(parts):
        span = pl.ds(k * some, some)
        pltpu.make_async_copy(buf.at[span], buf.at[span], sems.at[k]).wait()

        def body(i, carry):
            tile = dest_ref[i]
            slot = filled[tile]
            filled[tile] = slot + 1
            row = pl.multiple_of(slot * rows, rows)
            box_ref[tile, pl.ds(row, rows)] = buf[i].reshape(rows, COLS)
            return carry

        lax.fori_loop(k * some, (k + 1) * some, body, 0)
    for t in range(tiles):
        pltpu.make_async_copy(box_ref.at[t], out_ref.at[t], out_sems.at[t]).start()
    for t in range(tiles):
        pltpu.make_async_copy(box_ref.at[t], out_ref.at[t], out_sems.at[t]).wait()


def post(blocks, dest, note, fields, tiles, capacity, cost):
    slots = blocks.shape[0]
    rows = capacity * len(fields) * BPHI + NOTE
    return pl.pallas_call(
        functools.partial(post_kernel, fields, tiles, capacity),
        in_specs=[SMEM, VMEM, ANY],
        out_specs=HBM,
        out_shape=pltpu.HBM((tiles, rows, COLS), jnp.bfloat16),
        scratch_shapes=[
            pltpu.VMEM((tiles, rows, COLS), jnp.bfloat16),
            pltpu.VMEM((slots, len(fields), BPHI, COLS), jnp.bfloat16),
            pltpu.SMEM((tiles,), jnp.int32),
            pltpu.SemaphoreType.DMA((4,)),
            pltpu.SemaphoreType.DMA((tiles,)),
        ],
        compiler_params=params(),
        cost_estimate=cost,
        name="post",
    )(dest, note, *in_hbm(blocks))


def sort_kernel(planes, count, capacity, me_ref, slot_ref, weight_ref, note_ref, x_ref, *rest):
    outs, (buf, made, sems, out_sems) = rest[:-4], rest[-4:]
    tiles = buf.shape[0]
    per_plane = slot_ref.shape[0] // CG_DEV
    sliver = COLS // planes
    rows = count * BPHI
    side = CG_DEV * sliver
    me = me_ref[0]
    for d in range(planes):
        made[d, pl.ds(count * side, NOTE)] = note_ref[...]
    for t in range(tiles):
        pltpu.make_async_copy(x_ref.at[t], buf.at[t], sems.at[t]).start()
    for t in range(tiles):
        pltpu.make_async_copy(buf.at[t], buf.at[t], sems.at[t]).wait()

    def leave(f, d):
        span = pl.ds(f * side, side + (NOTE if f == count - 1 else 0))
        return pltpu.make_async_copy(made.at[d, span], outs[d].at[span], out_sems.at[f, d])

    def block(place, f):
        at = slot_ref[place]
        row = pl.multiple_of((at % capacity) * rows + f * BPHI, BPHI)
        return scaled(buf[at // capacity, pl.ds(row, BPHI)], weight_ref[place])

    for f in range(count):
        for j in range(per_plane // 2):

            def body(g, carry):
                even = block(2 * j * CG_DEV + g, f)
                odd = block((2 * j + 1) * CG_DEV + g, f)
                x = jnp.concatenate([even, odd], axis=0).T
                to = pl.ds(pl.multiple_of(f * side + g * sliver, sliver), sliver)
                for p in range(planes):
                    distance = (p - me + planes) % planes
                    made[distance, to, pl.ds(j * LANES, LANES)] = x[p * sliver : (p + 1) * sliver]
                return carry

            lax.fori_loop(0, CG_DEV, body, 0, unroll=4)
        for d in range(planes):
            leave(f, d).start()
    for f in range(count):
        for d in range(planes):
            leave(f, d).wait()


def sort(arrived, slot, weight, note, me, planes, count, capacity):
    cells = slot.shape[0] // CG_DEV * BPHI
    rows = count * CG_DEV * (COLS // planes) + NOTE
    return pl.pallas_call(
        functools.partial(sort_kernel, planes, count, capacity),
        in_specs=[SMEM, SMEM, SMEM, VMEM, ANY],
        out_specs=[HBM] * planes,
        out_shape=[pltpu.HBM((rows, cells), jnp.bfloat16)] * planes,
        scratch_shapes=[
            pltpu.VMEM(arrived.shape, jnp.bfloat16),
            pltpu.VMEM((planes, rows, cells), jnp.bfloat16),
            pltpu.SemaphoreType.DMA((arrived.shape[0],)),
            pltpu.SemaphoreType.DMA((count, planes)),
        ],
        compiler_params=params(),
        cost_estimate=LIGHT,
        name="sort",
    )(me, slot, weight, note, *in_hbm(arrived))


def mail_kernel(planes, tiles, capacity, slot_ref, *refs):
    ins, (out_ref, box_ref, buf, sems, out_sems) = refs[:planes], refs[planes:]
    slots = slot_ref.shape[1]
    sliver = box_ref.shape[1] // (planes * capacity)
    for d in range(planes):
        source = ins[d].at[pl.ds(0, slots * sliver)]
        pltpu.make_async_copy(source, buf.at[d], sems.at[d]).start()
    for d in range(planes):
        pltpu.make_async_copy(buf.at[d], buf.at[d], sems.at[d]).wait()

        def body(i, carry):
            to = slot_ref[d, i]
            row = pl.multiple_of((to % (planes * capacity)) * sliver, sliver)
            source = pl.ds(pl.multiple_of(i * sliver, sliver), sliver)
            box_ref[to // (planes * capacity), pl.ds(row, sliver)] = buf[d, source]
            return carry

        lax.fori_loop(0, slots, body, 0, unroll=4)
    for t in range(tiles):
        pltpu.make_async_copy(box_ref.at[t], out_ref.at[t], out_sems.at[t]).start()
    for t in range(tiles):
        pltpu.make_async_copy(box_ref.at[t], out_ref.at[t], out_sems.at[t]).wait()


def mail(parts, slot, tiles, capacity):
    planes, slots = slot.shape
    sliver = COLS // planes
    rows = planes * capacity * sliver
    return pl.pallas_call(
        functools.partial(mail_kernel, planes, tiles, capacity),
        in_specs=[SMEM] + [ANY] * planes,
        out_specs=HBM,
        out_shape=pltpu.HBM((tiles, rows, LANES), jnp.bfloat16),
        scratch_shapes=[
            pltpu.VMEM((tiles, rows, LANES), jnp.bfloat16),
            pltpu.VMEM((planes, slots * sliver, LANES), jnp.bfloat16),
            pltpu.SemaphoreType.DMA((planes,)),
            pltpu.SemaphoreType.DMA((tiles,)),
        ],
        compiler_params=params(),
        cost_estimate=SLOW,
        name="mail",
    )(slot, *in_hbm(*parts))


def load_basis(basis_hbm, basis, sems, spans):
    for j in spans:
        pltpu.make_async_copy(basis_hbm.at[j], basis.at[j], sems.at[j]).start()


def multiply(order, basis, out_hbm, rows, acc, basis_sems, sems, beside=None):
    wide = acc.shape[-1]
    copies = []
    for f, field in enumerate(order):
        for j in range(SPANS):
            n = len(copies)
            if f == 0:
                pltpu.make_async_copy(basis.at[j], basis.at[j], basis_sems.at[j]).wait()
            if beside is not None:
                beside(n)
            if n >= 2:
                copies[n - 2].wait()
            acc[n % 2] = jnp.dot(
                rows[f][...], basis[j], preferred_element_type=jnp.float32
            ).reshape(acc.shape[1:])
            copy = pltpu.make_async_copy(
                acc.at[n % 2], out_hbm.at[field, :, :, pl.ds(j * wide, wide)], sems.at[n % 2]
            )
            copy.start()
            copies.append(copy)
    for copy in copies[-2:]:
        copy.wait()


def load_rows(ins, take, rows, sems):
    cells = ins[0].shape[1]
    side = rows.shape[0]
    for d in range(len(ins)):
        to = rows.at[:, pl.ds(d * cells, cells)]
        pltpu.make_async_copy(ins[d].at[pl.ds(take * side, side)], to, sems.at[d]).start()


def wait_rows(planes, rows, sems):
    cells = rows.shape[1] // planes
    for d in range(planes):
        to = rows.at[:, pl.ds(d * cells, cells)]
        pltpu.make_async_copy(to, to, sems.at[d]).wait()


def rows_kernel(planes, take, field, chained, *refs):
    ins, basis_hbm = refs[:planes], refs[planes]
    out_hbm, rows, basis, acc, in_sems, basis_sems, out_sems = refs[planes + 1 + chained :]
    load_rows(ins, take, rows, in_sems)
    load_basis(basis_hbm, basis, basis_sems, range(1))
    wait_rows(planes, rows, in_sems)
    load_basis(basis_hbm, basis, basis_sems, range(1, SPANS))
    multiply((field,), basis, out_hbm, (rows,), acc, basis_sems, out_sems)


def box_kernel(planes, per_plane, capacity, *refs):
    slot_ref, box_hbm, basis_hbm, _, out_hbm = refs[:5]
    one, two, basis, acc, box, box_sems, basis_sems, out_sems = refs[5:]
    tiles = box.shape[0]
    sliver = COLS // planes
    for t in range(tiles):
        pltpu.make_async_copy(box_hbm.at[t], box.at[t], box_sems.at[t]).start()
    load_basis(basis_hbm, basis, basis_sems, range(1))
    for t in range(tiles):
        pltpu.make_async_copy(box.at[t], box.at[t], box_sems.at[t]).wait()
    load_basis(basis_hbm, basis, basis_sems, range(1, SPANS))

    def piece(d, place):
        at = slot_ref[d, place]
        row = pl.multiple_of((at % (planes * capacity)) * sliver, sliver)
        return box[at // (planes * capacity), pl.ds(row, sliver)]

    def gather(rows, cells, d):
        for j in range(per_plane // 2):
            lanes = pl.ds((d * per_plane + 2 * j) * BPHI, LANES)
            for g in range(CG_DEV):
                even = piece(d, 2 * j * CG_DEV + g)
                odd = piece(d, (2 * j + 1) * CG_DEV + g)
                both = jnp.concatenate([even[:, cells], odd[:, cells]], axis=1)
                rows[pl.ds(g * sliver, sliver), lanes] = both

    def beside(n):
        for d in range(planes):
            if n == d * SPANS // planes:
                gather(two, slice(BPHI, LANES), d)

    for d in range(planes):
        gather(one, slice(0, BPHI), d)
    multiply(PAIR, basis, out_hbm, (one, two), acc, basis_sems, out_sems, beside)


def transform(kernel, operands, specs, total, basis, planes, fields, extra, sems, cost, name):
    sliver = COLS // planes
    operands = operands + in_hbm(basis)
    specs = specs + [ANY]
    aliases = {}
    if total is not None:
        aliases = {len(operands): 0}
        operands, specs = operands + [total], specs + [ANY]
    rows = pltpu.VMEM((CG_DEV * sliver, NPHI), jnp.bfloat16)
    return pl.pallas_call(
        kernel,
        in_specs=specs,
        out_specs=HBM,
        out_shape=pltpu.HBM((FIELDS, CG_DEV, sliver, NPHI), jnp.float32),
        scratch_shapes=[rows] * fields
        + [
            pltpu.VMEM((SPANS, NPHI, NPHI // SPANS), jnp.bfloat16),
            pltpu.VMEM((2, CG_DEV, sliver, NPHI // SPANS), jnp.float32),
        ]
        + extra
        + [pltpu.SemaphoreType.DMA((sems,))]
        + [pltpu.SemaphoreType.DMA((SPANS,)), pltpu.SemaphoreType.DMA((2,))],
        input_output_aliases=aliases,
        compiler_params=params(),
        cost_estimate=cost,
        name=name,
    )(*operands)


def transform_rows(slabs, take, basis, total, field, cost):
    planes = len(slabs)
    kernel = functools.partial(rows_kernel, planes, take, field, int(total is not None))
    operands, specs = in_hbm(*slabs), [ANY] * planes
    return transform(kernel, operands, specs, total, basis, planes, 1, [], planes, cost, "rows")


def transform_box(box, slot, basis, total, per_plane, capacity):
    planes, tiles = slot.shape[0], box.shape[0]
    kernel = functools.partial(box_kernel, planes, per_plane, capacity)
    operands, specs = [slot] + in_hbm(box), [SMEM, ANY]
    extra = [pltpu.VMEM(box.shape, jnp.bfloat16)]
    return transform(kernel, operands, specs, total, basis, planes, 2, extra, tiles, LIGHT, "box")


def rank_of(dest):
    slots = dest.shape[-1]
    at = jnp.arange(slots, dtype=jnp.int32)
    same = (dest[..., :, None] == dest[..., None, :]) & (at[None, :] < at[:, None])
    return jnp.sum(same.astype(jnp.int32), axis=-1)


def as_note(dest, place_level, width):
    count = dest.size
    pad = -count % width
    each = (count + pad) // width
    codes = [jnp.pad(c.reshape(-1), (0, pad)).reshape(each, width) for c in (dest, place_level)]
    both = jnp.concatenate(codes, axis=0)
    return jnp.pad(both, ((0, NOTE - 2 * each), (0, 0))).astype(jnp.bfloat16)


def from_note(note, count):
    width = note.shape[2]
    each = -(-count // width)
    note = note.astype(jnp.float32).astype(jnp.int32)
    dest = note[:, :each].reshape(-1, each * width)[:, :count]
    place_level = note[:, each : 2 * each].reshape(-1, each * width)[:, :count]
    return dest, place_level


def local(blocks, levels, block_dest, block_phi, block_group):
    tiles = lax.axis_size("tile")
    planes = lax.axis_size("phi")
    tile = lax.axis_index("tile")
    plane = lax.axis_index("phi")
    slots = blocks.shape[0]
    per_plane = NPHI // BPHI // planes
    places = per_plane * CG_DEV
    capacity = 2 * slots // tiles
    me = plane.astype(jnp.int32).reshape(1)
    weight = 1.0 / jnp.left_shift(1, levels).astype(jnp.float32)
    place_iota = jnp.arange(places, dtype=jnp.int32)

    def over_phi(parts):
        moved = [parts[0]]
        for d in range(1, planes):
            pairs = [(s, (s + d) % planes) for s in range(planes)]
            moved.append(lax.ppermute(parts[d], "phi", pairs))
        return moved

    def over_tile(box):
        return lax.all_to_all(box, "tile", split_axis=0, concat_axis=0, tiled=True)

    def tie(value, *others):
        return lax.optimization_barrier((value,) + others)[0]

    place_level = levels * places + block_phi * CG_DEV + block_group
    distance = jnp.arange(planes, dtype=jnp.int32)[:, None]
    box_note = as_note(block_dest, place_level, COLS)
    box = post(blocks, block_dest, box_note, GROUPS[0], tiles, capacity, LIGHT)
    pieces = cut(blocks, weight, as_note(block_dest, place_level, LANES), me, planes)
    source = tie(blocks, pieces[0])
    next_box = post(source, block_dest, box_note, GROUPS[1], tiles, capacity, SLOWER)

    back = (plane - jnp.arange(planes, dtype=jnp.int32)) % planes
    basis = rotated_basis(NPHI, back)

    first = over_tile(box)
    sent = over_phi(pieces)
    second = over_tile(tie(next_box, first, basis))

    got_dest, got_code = from_note(first[:, -NOTE:], slots)
    got_slot = jnp.arange(tiles, dtype=jnp.int32)[:, None] * capacity + rank_of(got_dest)
    here = (got_dest == tile)[..., None] & ((got_code % places)[..., None] == place_iota)
    slot = jnp.sum(jnp.where(here, got_slot[..., None], 0), axis=(0, 1))
    level = jnp.sum(jnp.where(here, (got_code // places)[..., None], 0), axis=(0, 1))
    got_weight = 1.0 / jnp.left_shift(1, level).astype(jnp.float32)
    note = as_note(got_dest, got_code, per_plane * BPHI)

    early = sort(first, slot, got_weight, note, me, planes, 2, capacity)
    sent = list(lax.optimization_barrier((tuple(sent), early[0]))[0])
    early = over_phi(early)

    dest, _ = from_note(jnp.stack([part[-NOTE:] for part in sent]), slots)
    out_slot = (dest * planes + distance) * capacity + rank_of(dest)

    outbox = mail(sent, out_slot, tiles, capacity)
    last = over_tile(tie(outbox, second))
    rest = sort(second, slot, got_weight, note, me, planes, 1, capacity)
    early = [tie(early[0], *rest)] + early[1:]
    rest = over_phi(rest)

    from_dest, from_code = from_note(jnp.stack([part[-NOTE:] for part in early]), tiles * slots)
    from_dest = from_dest.reshape(planes, tiles, slots)
    from_place = from_code.reshape(planes, tiles, slots) % places
    start = jnp.arange(tiles, dtype=jnp.int32)[None, :, None] * planes + distance[..., None]
    from_slot = start * capacity + rank_of(from_dest)
    here = (from_dest == tile)[..., None] & (from_place[..., None] == place_iota)
    routed = jnp.sum(jnp.where(here, from_slot[..., None], 0), axis=(1, 2))

    total = transform_rows(early, 0, basis, None, GROUPS[0][0], SLOWER)
    total = transform_rows(early, 1, basis, total, GROUPS[0][1], SLOWER)
    total = transform_box(last, routed, basis, total, per_plane, capacity)
    return transform_rows(rest, 0, basis, total, GROUPS[1][0], LIGHT)


def solution(mesh):
    in_specs = (
        P(("tile", "phi"), None, None, None),
        P(("tile", "phi")),
        P(("tile", "phi")),
        P(("tile", "phi")),
        P(("tile", "phi")),
    )
    out_specs = P(None, "tile", "phi", None)
    return jax.shard_map(local, mesh=mesh, in_specs=in_specs, out_specs=out_specs, check_vma=False)
```

```python
import functools
import math

import jax
import jax.numpy as jnp
from jax import lax
from jax.experimental import pallas as pl
from jax.experimental.pallas import tpu as pltpu
from jax.sharding import PartitionSpec as P

FIELDS = 5
NPHI = 2048
BPHI = 64
COLS = 256
CG_DEV = 8
LANES = 128
NOTE = 16
PAIR = (0, 1)
GROUPS = ((2, 3), (4,))
VMEM_BYTES = 32 * 1024 * 1024
SPANS = 4
LIGHT = pl.CostEstimate(flops=0, bytes_accessed=0, transcendentals=0)
SLOW = pl.CostEstimate(flops=20_000_000_000, bytes_accessed=0, transcendentals=0)
SLOWER = pl.CostEstimate(flops=30_000_000_000, bytes_accessed=0, transcendentals=0)

ANY = pl.BlockSpec(memory_space=pl.ANY)
HBM = pl.BlockSpec(memory_space=pltpu.HBM)
SMEM = pl.BlockSpec(memory_space=pltpu.SMEM)
VMEM = pl.BlockSpec(memory_space=pltpu.VMEM)


def rotated_basis(length, back):
    planes = back.shape[0]
    per = length // planes
    column = jnp.arange(length, dtype=jnp.int32)
    half = length // 2
    mode = jnp.where(column <= half, column, column - half)
    coarse = (back[:, None] * per + jnp.arange(0, per, BPHI, dtype=jnp.int32)[None, :]).reshape(-1)
    fine = jnp.arange(BPHI, dtype=jnp.int32)

    def angle(row):
        phase = row[:, None] * mode[None, :] % length
        return phase.astype(jnp.float32) * jnp.float32(2.0 * math.pi / length)

    even = (column <= half)[None, :]
    scale = jnp.float32(1.0 / math.sqrt(length))
    far, near = angle(coarse), angle(fine)
    by_cos = jnp.where(even, jnp.cos(far), jnp.sin(far)) * scale
    by_sin = jnp.where(even, -jnp.sin(far), jnp.cos(far)) * scale
    near_cos, near_sin = jnp.cos(near), jnp.sin(near)

    def spans(x):
        return x.reshape(x.shape[0], SPANS, length // SPANS).transpose(1, 0, 2)

    by_cos, by_sin = spans(by_cos)[:, :, None], spans(by_sin)[:, :, None]
    near_cos, near_sin = spans(near_cos)[:, None], spans(near_sin)[:, None]
    by_cos, by_sin, near_cos, near_sin = lax.optimization_barrier((by_cos, by_sin, near_cos, near_sin))
    table = by_cos * near_cos + by_sin * near_sin
    return table.reshape(SPANS, length, length // SPANS).astype(jnp.bfloat16)


def in_hbm(*arrays):
    return [pltpu.with_memory_space_constraint(a, pltpu.HBM) for a in arrays]


def params():
    return pltpu.CompilerParams(vmem_limit_bytes=VMEM_BYTES)


def scaled(block, weight):
    return block * jnp.full((1, 1), weight, jnp.float32).astype(jnp.bfloat16)


def cut_kernel(planes, me_ref, weight_ref, note_ref, x_ref, *refs):
    outs, (buf, made, sems, out_sems) = refs[:planes], refs[planes:]
    slots = buf.shape[0]
    sliver = COLS // planes
    parts = sems.shape[0]
    some = slots // parts
    me = me_ref[0]
    for k in range(parts):
        span = pl.ds(k * some, some)
        source = x_ref.at[span, pl.ds(PAIR[0], 2)]
        pltpu.make_async_copy(source, buf.at[span], sems.at[k]).start()
    for d in range(planes):
        made[d, pl.ds(slots * sliver, NOTE)] = note_ref[...]

    def leave(k, d):
        rows = some * sliver + (NOTE if k == parts - 1 else 0)
        span = pl.ds(k * some * sliver, rows)
        return pltpu.make_async_copy(made.at[d, span], outs[d].at[span], out_sems.at[k, d])

    for k in range(parts):
        span = pl.ds(k * some, some)
        pltpu.make_async_copy(buf.at[span], buf.at[span], sems.at[k]).wait()

        def body(i, carry):
            x = scaled(buf[i].reshape(LANES, COLS), weight_ref[i]).T
            to = pl.ds(pl.multiple_of(i * sliver, sliver), sliver)
            for p in range(planes):
                made[(p - me + planes) % planes, to] = x[p * sliver : (p + 1) * sliver]
            return carry

        lax.fori_loop(k * some, (k + 1) * some, body, 0, unroll=4)
        for d in range(planes):
            leave(k, d).start()
    for k in range(parts):
        for d in range(planes):
            leave(k, d).wait()


def cut(blocks, weight, note, me, planes):
    slots = blocks.shape[0]
    parts = 4
    rows = slots * (COLS // planes) + NOTE
    return pl.pallas_call(
        functools.partial(cut_kernel, planes),
        in_specs=[SMEM, SMEM, VMEM, ANY],
        out_specs=[HBM] * planes,
        out_shape=[pltpu.HBM((rows, LANES), jnp.bfloat16)] * planes,
        scratch_shapes=[
            pltpu.VMEM((slots, 2, BPHI, COLS), jnp.bfloat16),
            pltpu.VMEM((planes, rows, LANES), jnp.bfloat16),
            pltpu.SemaphoreType.DMA((parts,)),
            pltpu.SemaphoreType.DMA((parts, planes)),
        ],
        compiler_params=params(),
        cost_estimate=LIGHT,
        name="cut",
    )(me, weight, note, *in_hbm(blocks))


def post_kernel(
    fields, tiles, capacity, dest_ref, note_ref, x_ref, out_ref, box_ref, buf, filled, sems, out_sems
):
    slots = dest_ref.shape[0]
    count = len(fields)
    rows = count * BPHI
    parts = sems.shape[0]
    some = slots // parts
    for k in range(parts):
        span = pl.ds(k * some, some)
        source = x_ref.at[span, pl.ds(fields[0], count)]
        pltpu.make_async_copy(source, buf.at[span], sems.at[k]).start()
    for t in range(tiles):
        filled[t] = 0
        box_ref[t, pl.ds(capacity * rows, NOTE)] = note_ref[...]
    for k in range(parts):
        span = pl.ds(k * some, some)
        pltpu.make_async_copy(buf.at[span], buf.at[span], sems.at[k]).wait()

        def body(i, carry):
            tile = dest_ref[i]
            slot = filled[tile]
            filled[tile] = slot + 1
            row = pl.multiple_of(slot * rows, rows)
            box_ref[tile, pl.ds(row, rows)] = buf[i].reshape(rows, COLS)
            return carry

        lax.fori_loop(k * some, (k + 1) * some, body, 0)
    for t in range(tiles):
        pltpu.make_async_copy(box_ref.at[t], out_ref.at[t], out_sems.at[t]).start()
    for t in range(tiles):
        pltpu.make_async_copy(box_ref.at[t], out_ref.at[t], out_sems.at[t]).wait()


def post(blocks, dest, note, fields, tiles, capacity, cost):
    slots = blocks.shape[0]
    rows = capacity * len(fields) * BPHI + NOTE
    return pl.pallas_call(
        functools.partial(post_kernel, fields, tiles, capacity),
        in_specs=[SMEM, VMEM, ANY],
        out_specs=HBM,
        out_shape=pltpu.HBM((tiles, rows, COLS), jnp.bfloat16),
        scratch_shapes=[
            pltpu.VMEM((tiles, rows, COLS), jnp.bfloat16),
            pltpu.VMEM((slots, len(fields), BPHI, COLS), jnp.bfloat16),
            pltpu.SMEM((tiles,), jnp.int32),
            pltpu.SemaphoreType.DMA((4,)),
            pltpu.SemaphoreType.DMA((tiles,)),
        ],
        compiler_params=params(),
        cost_estimate=cost,
        name="post",
    )(dest, note, *in_hbm(blocks))


def sort_kernel(planes, count, capacity, me_ref, slot_ref, weight_ref, note_ref, x_ref, *rest):
    outs, (buf, made, sems, out_sems) = rest[:-4], rest[-4:]
    tiles = buf.shape[0]
    per_plane = slot_ref.shape[0] // CG_DEV
    sliver = COLS // planes
    rows = count * BPHI
    side = CG_DEV * sliver
    me = me_ref[0]
    for d in range(planes):
        made[d, pl.ds(count * side, NOTE)] = note_ref[...]
    for t in range(tiles):
        pltpu.make_async_copy(x_ref.at[t], buf.at[t], sems.at[t]).start()
    for t in range(tiles):
        pltpu.make_async_copy(buf.at[t], buf.at[t], sems.at[t]).wait()

    def leave(f, d):
        span = pl.ds(f * side, side + (NOTE if f == count - 1 else 0))
        return pltpu.make_async_copy(made.at[d, span], outs[d].at[span], out_sems.at[f, d])

    def block(place, f):
        at = slot_ref[place]
        row = pl.multiple_of((at % capacity) * rows + f * BPHI, BPHI)
        return scaled(buf[at // capacity, pl.ds(row, BPHI)], weight_ref[place])

    for f in range(count):
        for j in range(per_plane // 2):

            def body(g, carry):
                even = block(2 * j * CG_DEV + g, f)
                odd = block((2 * j + 1) * CG_DEV + g, f)
                x = jnp.concatenate([even, odd], axis=0).T
                to = pl.ds(pl.multiple_of(f * side + g * sliver, sliver), sliver)
                for p in range(planes):
                    distance = (p - me + planes) % planes
                    made[distance, to, pl.ds(j * LANES, LANES)] = x[p * sliver : (p + 1) * sliver]
                return carry

            lax.fori_loop(0, CG_DEV, body, 0, unroll=4)
        for d in range(planes):
            leave(f, d).start()
    for f in range(count):
        for d in range(planes):
            leave(f, d).wait()


def sort(arrived, slot, weight, note, me, planes, count, capacity):
    cells = slot.shape[0] // CG_DEV * BPHI
    rows = count * CG_DEV * (COLS // planes) + NOTE
    return pl.pallas_call(
        functools.partial(sort_kernel, planes, count, capacity),
        in_specs=[SMEM, SMEM, SMEM, VMEM, ANY],
        out_specs=[HBM] * planes,
        out_shape=[pltpu.HBM((rows, cells), jnp.bfloat16)] * planes,
        scratch_shapes=[
            pltpu.VMEM(arrived.shape, jnp.bfloat16),
            pltpu.VMEM((planes, rows, cells), jnp.bfloat16),
            pltpu.SemaphoreType.DMA((arrived.shape[0],)),
            pltpu.SemaphoreType.DMA((count, planes)),
        ],
        compiler_params=params(),
        cost_estimate=LIGHT,
        name="sort",
    )(me, slot, weight, note, *in_hbm(arrived))


def mail_kernel(planes, tiles, capacity, slot_ref, *refs):
    ins, (out_ref, box_ref, buf, sems, out_sems) = refs[:planes], refs[planes:]
    slots = slot_ref.shape[1]
    sliver = box_ref.shape[1] // (planes * capacity)
    for d in range(planes):
        source = ins[d].at[pl.ds(0, slots * sliver)]
        pltpu.make_async_copy(source, buf.at[d], sems.at[d]).start()
    for d in range(planes):
        pltpu.make_async_copy(buf.at[d], buf.at[d], sems.at[d]).wait()

        def body(i, carry):
            to = slot_ref[d, i]
            row = pl.multiple_of((to % (planes * capacity)) * sliver, sliver)
            source = pl.ds(pl.multiple_of(i * sliver, sliver), sliver)
            box_ref[to // (planes * capacity), pl.ds(row, sliver)] = buf[d, source]
            return carry

        lax.fori_loop(0, slots, body, 0, unroll=4)
    for t in range(tiles):
        pltpu.make_async_copy(box_ref.at[t], out_ref.at[t], out_sems.at[t]).start()
    for t in range(tiles):
        pltpu.make_async_copy(box_ref.at[t], out_ref.at[t], out_sems.at[t]).wait()


def mail(parts, slot, tiles, capacity):
    planes, slots = slot.shape
    sliver = COLS // planes
    rows = planes * capacity * sliver
    return pl.pallas_call(
        functools.partial(mail_kernel, planes, tiles, capacity),
        in_specs=[SMEM] + [ANY] * planes,
        out_specs=HBM,
        out_shape=pltpu.HBM((tiles, rows, LANES), jnp.bfloat16),
        scratch_shapes=[
            pltpu.VMEM((tiles, rows, LANES), jnp.bfloat16),
            pltpu.VMEM((planes, slots * sliver, LANES), jnp.bfloat16),
            pltpu.SemaphoreType.DMA((planes,)),
            pltpu.SemaphoreType.DMA((tiles,)),
        ],
        compiler_params=params(),
        cost_estimate=SLOW,
        name="mail",
    )(slot, *in_hbm(*parts))


def load_basis(basis_hbm, basis, sems, spans):
    for j in spans:
        pltpu.make_async_copy(basis_hbm.at[j], basis.at[j], sems.at[j]).start()


def multiply(order, basis, out_hbm, rows, acc, basis_sems, sems, beside=None):
    wide = acc.shape[-1]
    copies = []
    for f, field in enumerate(order):
        for j in range(SPANS):
            n = len(copies)
            if f == 0:
                pltpu.make_async_copy(basis.at[j], basis.at[j], basis_sems.at[j]).wait()
            if beside is not None:
                beside(n)
            if n >= 2:
                copies[n - 2].wait()
            acc[n % 2] = jnp.dot(
                rows[f][...], basis[j], preferred_element_type=jnp.float32
            ).reshape(acc.shape[1:])
            copy = pltpu.make_async_copy(
                acc.at[n % 2], out_hbm.at[field, :, :, pl.ds(j * wide, wide)], sems.at[n % 2]
            )
            copy.start()
            copies.append(copy)
    for copy in copies[-2:]:
        copy.wait()


def load_rows(ins, take, rows, sems):
    cells = ins[0].shape[1]
    side = rows.shape[0]
    for d in range(len(ins)):
        to = rows.at[:, pl.ds(d * cells, cells)]
        pltpu.make_async_copy(ins[d].at[pl.ds(take * side, side)], to, sems.at[d]).start()


def wait_rows(planes, rows, sems):
    cells = rows.shape[1] // planes
    for d in range(planes):
        to = rows.at[:, pl.ds(d * cells, cells)]
        pltpu.make_async_copy(to, to, sems.at[d]).wait()


def rows_kernel(planes, take, field, chained, *refs):
    ins, basis_hbm = refs[:planes], refs[planes]
    out_hbm, rows, basis, acc, in_sems, basis_sems, out_sems = refs[planes + 1 + chained :]
    load_rows(ins, take, rows, in_sems)
    load_basis(basis_hbm, basis, basis_sems, range(1))
    wait_rows(planes, rows, in_sems)
    load_basis(basis_hbm, basis, basis_sems, range(1, SPANS))
    multiply((field,), basis, out_hbm, (rows,), acc, basis_sems, out_sems)


def box_kernel(planes, per_plane, capacity, *refs):
    slot_ref, box_hbm, basis_hbm, _, out_hbm = refs[:5]
    one, two, basis, acc, box, box_sems, basis_sems, out_sems = refs[5:]
    tiles = box.shape[0]
    sliver = COLS // planes
    for t in range(tiles):
        pltpu.make_async_copy(box_hbm.at[t], box.at[t], box_sems.at[t]).start()
    load_basis(basis_hbm, basis, basis_sems, range(1))
    for t in range(tiles):
        pltpu.make_async_copy(box.at[t], box.at[t], box_sems.at[t]).wait()
    load_basis(basis_hbm, basis, basis_sems, range(1, SPANS))

    def piece(d, place):
        at = slot_ref[d, place]
        row = pl.multiple_of((at % (planes * capacity)) * sliver, sliver)
        return box[at // (planes * capacity), pl.ds(row, sliver)]

    def gather(rows, cells, d):
        for j in range(per_plane // 2):
            lanes = pl.ds((d * per_plane + 2 * j) * BPHI, LANES)
            for g in range(CG_DEV):
                even = piece(d, 2 * j * CG_DEV + g)
                odd = piece(d, (2 * j + 1) * CG_DEV + g)
                both = jnp.concatenate([even[:, cells], odd[:, cells]], axis=1)
                rows[pl.ds(g * sliver, sliver), lanes] = both

    def beside(n):
        for d in range(planes):
            if n == d * SPANS // planes:
                gather(two, slice(BPHI, LANES), d)

    for d in range(planes):
        gather(one, slice(0, BPHI), d)
    multiply(PAIR, basis, out_hbm, (one, two), acc, basis_sems, out_sems, beside)


def transform(kernel, operands, specs, total, basis, planes, fields, extra, sems, cost, name):
    sliver = COLS // planes
    operands = operands + in_hbm(basis)
    specs = specs + [ANY]
    aliases = {}
    if total is not None:
        aliases = {len(operands): 0}
        operands, specs = operands + [total], specs + [ANY]
    rows = pltpu.VMEM((CG_DEV * sliver, NPHI), jnp.bfloat16)
    return pl.pallas_call(
        kernel,
        in_specs=specs,
        out_specs=HBM,
        out_shape=pltpu.HBM((FIELDS, CG_DEV, sliver, NPHI), jnp.float32),
        scratch_shapes=[rows] * fields
        + [
            pltpu.VMEM((SPANS, NPHI, NPHI // SPANS), jnp.bfloat16),
            pltpu.VMEM((2, CG_DEV, sliver, NPHI // SPANS), jnp.float32),
        ]
        + extra
        + [pltpu.SemaphoreType.DMA((sems,))]
        + [pltpu.SemaphoreType.DMA((SPANS,)), pltpu.SemaphoreType.DMA((2,))],
        input_output_aliases=aliases,
        compiler_params=params(),
        cost_estimate=cost,
        name=name,
    )(*operands)


def transform_rows(slabs, take, basis, total, field, cost):
    planes = len(slabs)
    kernel = functools.partial(rows_kernel, planes, take, field, int(total is not None))
    operands, specs = list(slabs), [ANY] * planes
    return transform(kernel, operands, specs, total, basis, planes, 1, [], planes, cost, "rows")


def transform_box(box, slot, basis, total, per_plane, capacity):
    planes, tiles = slot.shape[0], box.shape[0]
    kernel = functools.partial(box_kernel, planes, per_plane, capacity)
    operands, specs = [slot] + in_hbm(box), [SMEM, ANY]
    extra = [pltpu.VMEM(box.shape, jnp.bfloat16)]
    return transform(kernel, operands, specs, total, basis, planes, 2, extra, tiles, LIGHT, "box")


def rank_of(dest):
    slots = dest.shape[-1]
    at = jnp.arange(slots, dtype=jnp.int32)
    same = (dest[..., :, None] == dest[..., None, :]) & (at[None, :] < at[:, None])
    return jnp.sum(same.astype(jnp.int32), axis=-1)


def as_note(dest, place_level, width):
    count = dest.size
    each = -(-count // width)
    row = jnp.arange(NOTE, dtype=jnp.int32)[:, None]
    if each > 1:
        codes = [c.reshape(-1) for c in (dest, place_level)]
        codes = [jnp.pad(c, (0, each * width - count)).reshape(each, width) for c in codes]
        both = jnp.concatenate(codes, axis=0)
        return jnp.pad(both, ((0, NOTE - 2 * each), (0, 0))).astype(jnp.bfloat16)
    wide = [jnp.pad(c.reshape(1, -1), ((0, 0), (0, width - count))) for c in (dest, place_level)]
    return jnp.where(row == 0, wide[0], jnp.where(row == 1, wide[1], 0)).astype(jnp.bfloat16)


def from_note(note, count):
    width = note.shape[2]
    each = -(-count // width)
    note = note.astype(jnp.float32).astype(jnp.int32)
    dest = note[:, :each].reshape(-1, each * width)[:, :count]
    place_level = note[:, each : 2 * each].reshape(-1, each * width)[:, :count]
    return dest, place_level


def local(blocks, levels, block_dest, block_phi, block_group):
    tiles = lax.axis_size("tile")
    planes = lax.axis_size("phi")
    tile = lax.axis_index("tile")
    plane = lax.axis_index("phi")
    slots = blocks.shape[0]
    per_plane = NPHI // BPHI // planes
    places = per_plane * CG_DEV
    capacity = 2 * slots // tiles
    me = plane.astype(jnp.int32).reshape(1)
    weight = 1.0 / jnp.left_shift(1, levels).astype(jnp.float32)
    place_iota = jnp.arange(places, dtype=jnp.int32)

    def over_phi(parts):
        moved = [parts[0]]
        for d in range(1, planes):
            pairs = [(s, (s + d) % planes) for s in range(planes)]
            moved.append(lax.ppermute(parts[d], "phi", pairs))
        return moved

    def over_tile(box):
        return lax.all_to_all(box, "tile", split_axis=0, concat_axis=0, tiled=True)

    def tie(value, *others):
        return lax.optimization_barrier((value,) + others)[0]

    place_level = levels * places + block_phi * CG_DEV + block_group
    distance = jnp.arange(planes, dtype=jnp.int32)[:, None]
    box_note = as_note(block_dest, place_level, COLS)
    box = post(blocks, block_dest, box_note, GROUPS[0], tiles, capacity, LIGHT)
    pieces = cut(blocks, weight, as_note(block_dest, place_level, LANES), me, planes)
    source = tie(blocks, pieces[0])
    next_box = post(source, block_dest, box_note, GROUPS[1], tiles, capacity, SLOWER)

    back = (plane - jnp.arange(planes, dtype=jnp.int32)) % planes
    basis = rotated_basis(NPHI, back)

    first = over_tile(box)
    sent = over_phi(pieces)
    second = over_tile(tie(next_box, first, basis))

    got_dest, got_code = from_note(first[:, -NOTE:], slots)
    got_slot = jnp.arange(tiles, dtype=jnp.int32)[:, None] * capacity + rank_of(got_dest)
    here = (got_dest == tile)[..., None] & ((got_code % places)[..., None] == place_iota)
    slot = jnp.sum(jnp.where(here, got_slot[..., None], 0), axis=(0, 1))
    level = jnp.sum(jnp.where(here, (got_code // places)[..., None], 0), axis=(0, 1))
    got_weight = 1.0 / jnp.left_shift(1, level).astype(jnp.float32)
    note = as_note(got_dest, got_code, per_plane * BPHI)

    early = sort(first, slot, got_weight, note, me, planes, 2, capacity)
    sent = list(lax.optimization_barrier((tuple(sent), early[0]))[0])
    early = over_phi(early)

    dest, _ = from_note(jnp.stack([part[-NOTE:] for part in sent]), slots)
    out_slot = (dest * planes + distance) * capacity + rank_of(dest)

    outbox = mail(sent, out_slot, tiles, capacity)
    last = over_tile(tie(outbox, second))
    rest = sort(second, slot, got_weight, note, me, planes, 1, capacity)
    early = [tie(early[0], *rest)] + early[1:]
    rest = over_phi(rest)

    from_dest, from_code = from_note(jnp.stack([part[-NOTE:] for part in early]), tiles * slots)
    from_dest = from_dest.reshape(planes, tiles, slots)
    from_place = from_code.reshape(planes, tiles, slots) % places
    start = jnp.arange(tiles, dtype=jnp.int32)[None, :, None] * planes + distance[..., None]
    from_slot = start * capacity + rank_of(from_dest)
    here = (from_dest == tile)[..., None] & (from_place[..., None] == place_iota)
    routed = jnp.sum(jnp.where(here, from_slot[..., None], 0), axis=(1, 2))

    total = transform_rows(early, 0, basis, None, GROUPS[0][0], SLOWER)
    total = transform_rows(early, 1, basis, total, GROUPS[0][1], SLOWER)
    total = transform_box(last, routed, basis, total, per_plane, capacity)
    return transform_rows(rest, 0, basis, total, GROUPS[1][0], LIGHT)


def solution(mesh):
    in_specs = (
        P(("tile", "phi"), None, None, None),
        P(("tile", "phi")),
        P(("tile", "phi")),
        P(("tile", "phi")),
        P(("tile", "phi")),
    )
    out_specs = P(None, "tile", "phi", None)
    return jax.shard_map(local, mesh=mesh, in_specs=in_specs, out_specs=out_specs, check_vma=False)
```

```python
import functools
import math

import jax
import jax.numpy as jnp
from jax import lax
from jax.experimental import pallas as pl
from jax.experimental.pallas import tpu as pltpu
from jax.sharding import PartitionSpec as P

FIELDS = 5
NPHI = 2048
BPHI = 64
COLS = 256
CG_DEV = 8
LANES = 128
NOTE = 16
PAIR = (0, 1)
GROUPS = ((2, 3), (4,))
VMEM_BYTES = 32 * 1024 * 1024
SPANS = 4
LIGHT = pl.CostEstimate(flops=0, bytes_accessed=0, transcendentals=0)
SLOW = pl.CostEstimate(flops=20_000_000_000, bytes_accessed=0, transcendentals=0)
SLOWER = pl.CostEstimate(flops=30_000_000_000, bytes_accessed=0, transcendentals=0)

ANY = pl.BlockSpec(memory_space=pl.ANY)
HBM = pl.BlockSpec(memory_space=pltpu.HBM)
SMEM = pl.BlockSpec(memory_space=pltpu.SMEM)
VMEM = pl.BlockSpec(memory_space=pltpu.VMEM)


def rotated_basis(length, back):
    planes = back.shape[0]
    per = length // planes
    column = jnp.arange(length, dtype=jnp.int32)
    half = length // 2
    mode = jnp.where(column <= half, column, column - half)
    coarse = (back[:, None] * per + jnp.arange(0, per, BPHI, dtype=jnp.int32)[None, :]).reshape(-1)
    fine = jnp.arange(BPHI, dtype=jnp.int32)

    def angle(row):
        phase = row[:, None] * mode[None, :] % length
        return phase.astype(jnp.float32) * jnp.float32(2.0 * math.pi / length)

    even = (column <= half)[None, :]
    scale = jnp.float32(1.0 / math.sqrt(length))
    far, near = angle(coarse), angle(fine)
    by_cos = jnp.where(even, jnp.cos(far), jnp.sin(far)) * scale
    by_sin = jnp.where(even, -jnp.sin(far), jnp.cos(far)) * scale
    near_cos, near_sin = jnp.cos(near), jnp.sin(near)

    def spans(x):
        return x.reshape(x.shape[0], SPANS, length // SPANS).transpose(1, 0, 2)

    by_cos, by_sin = spans(by_cos)[:, :, None], spans(by_sin)[:, :, None]
    near_cos, near_sin = spans(near_cos)[:, None], spans(near_sin)[:, None]
    by_cos, by_sin, near_cos, near_sin = lax.optimization_barrier((by_cos, by_sin, near_cos, near_sin))
    table = by_cos * near_cos + by_sin * near_sin
    return table.reshape(SPANS, length, length // SPANS).astype(jnp.bfloat16)


def in_hbm(*arrays):
    return [pltpu.with_memory_space_constraint(a, pltpu.HBM) for a in arrays]


def params():
    return pltpu.CompilerParams(vmem_limit_bytes=VMEM_BYTES)


def scaled(block, weight):
    return block * jnp.full((1, 1), weight, jnp.float32).astype(jnp.bfloat16)


def cut_kernel(planes, me_ref, weight_ref, note_ref, x_ref, *refs):
    outs, (buf, made, sems, out_sems) = refs[:planes], refs[planes:]
    slots = buf.shape[0]
    sliver = COLS // planes
    parts = sems.shape[0]
    some = slots // parts
    me = me_ref[0]
    for k in range(parts):
        span = pl.ds(k * some, some)
        source = x_ref.at[span, pl.ds(PAIR[0], 2)]
        pltpu.make_async_copy(source, buf.at[span], sems.at[k]).start()
    for d in range(planes):
        made[d, pl.ds(slots * sliver, NOTE)] = note_ref[...]

    def leave(k, d):
        rows = some * sliver + (NOTE if k == parts - 1 else 0)
        span = pl.ds(k * some * sliver, rows)
        return pltpu.make_async_copy(made.at[d, span], outs[d].at[span], out_sems.at[k, d])

    for k in range(parts):
        span = pl.ds(k * some, some)
        pltpu.make_async_copy(buf.at[span], buf.at[span], sems.at[k]).wait()

        def body(i, carry):
            x = scaled(buf[i].reshape(LANES, COLS), weight_ref[i]).T
            to = pl.ds(pl.multiple_of(i * sliver, sliver), sliver)
            for p in range(planes):
                made[(p - me + planes) % planes, to] = x[p * sliver : (p + 1) * sliver]
            return carry

        lax.fori_loop(k * some, (k + 1) * some, body, 0, unroll=4)
        for d in range(planes):
            leave(k, d).start()
    for k in range(parts):
        for d in range(planes):
            leave(k, d).wait()


def cut(blocks, weight, note, me, planes):
    slots = blocks.shape[0]
    parts = 4
    rows = slots * (COLS // planes) + NOTE
    return pl.pallas_call(
        functools.partial(cut_kernel, planes),
        in_specs=[SMEM, SMEM, VMEM, ANY],
        out_specs=[HBM] * planes,
        out_shape=[pltpu.HBM((rows, LANES), jnp.bfloat16)] * planes,
        scratch_shapes=[
            pltpu.VMEM((slots, 2, BPHI, COLS), jnp.bfloat16),
            pltpu.VMEM((planes, rows, LANES), jnp.bfloat16),
            pltpu.SemaphoreType.DMA((parts,)),
            pltpu.SemaphoreType.DMA((parts, planes)),
        ],
        compiler_params=params(),
        cost_estimate=LIGHT,
        name="cut",
    )(me, weight, note, *in_hbm(blocks))


def post_kernel(
    fields, tiles, capacity, dest_ref, note_ref, x_ref, out_ref, box_ref, buf, filled, sems, out_sems
):
    slots = dest_ref.shape[0]
    count = len(fields)
    rows = count * BPHI
    parts = sems.shape[0]
    some = slots // parts
    for k in range(parts):
        span = pl.ds(k * some, some)
        source = x_ref.at[span, pl.ds(fields[0], count)]
        pltpu.make_async_copy(source, buf.at[span], sems.at[k]).start()
    for t in range(tiles):
        filled[t] = 0
        box_ref[t, pl.ds(capacity * rows, NOTE)] = note_ref[...]
    for k in range(parts):
        span = pl.ds(k * some, some)
        pltpu.make_async_copy(buf.at[span], buf.at[span], sems.at[k]).wait()

        def body(i, carry):
            tile = dest_ref[i]
            slot = filled[tile]
            filled[tile] = slot + 1
            row = pl.multiple_of(slot * rows, rows)
            box_ref[tile, pl.ds(row, rows)] = buf[i].reshape(rows, COLS)
            return carry

        lax.fori_loop(k * some, (k + 1) * some, body, 0)
    half = capacity // 2 * rows

    def leave(t, k, at, size):
        span = pl.ds(at, size)
        return pltpu.make_async_copy(box_ref.at[t, span], out_ref.at[t, span], out_sems.at[t, k])

    def upper(t, act):
        @pl.when(filled[t] > capacity // 2)
        def _():
            act(leave(t, 1, half, half + NOTE))

        @pl.when(filled[t] <= capacity // 2)
        def _():
            act(leave(t, 2, capacity * rows, NOTE))

    for t in range(tiles):
        leave(t, 0, 0, half).start()
        upper(t, lambda copy: copy.start())
    for t in range(tiles):
        leave(t, 0, 0, half).wait()
        upper(t, lambda copy: copy.wait())


def post(blocks, dest, note, fields, tiles, capacity, cost):
    slots = blocks.shape[0]
    rows = capacity * len(fields) * BPHI + NOTE
    return pl.pallas_call(
        functools.partial(post_kernel, fields, tiles, capacity),
        in_specs=[SMEM, VMEM, ANY],
        out_specs=HBM,
        out_shape=pltpu.HBM((tiles, rows, COLS), jnp.bfloat16),
        scratch_shapes=[
            pltpu.VMEM((tiles, rows, COLS), jnp.bfloat16),
            pltpu.VMEM((slots, len(fields), BPHI, COLS), jnp.bfloat16),
            pltpu.SMEM((tiles,), jnp.int32),
            pltpu.SemaphoreType.DMA((4,)),
            pltpu.SemaphoreType.DMA((tiles, 3)),
        ],
        compiler_params=params(),
        cost_estimate=cost,
        name="post",
    )(dest, note, *in_hbm(blocks))


def sort_kernel(planes, count, capacity, me_ref, slot_ref, weight_ref, note_ref, x_ref, *rest):
    outs, (buf, made, sems, out_sems) = rest[:-4], rest[-4:]
    tiles = buf.shape[0]
    per_plane = slot_ref.shape[0] // CG_DEV
    sliver = COLS // planes
    rows = count * BPHI
    side = CG_DEV * sliver
    me = me_ref[0]
    for d in range(planes):
        made[d, pl.ds(count * side, NOTE)] = note_ref[...]
    for t in range(tiles):
        pltpu.make_async_copy(x_ref.at[t], buf.at[t], sems.at[t]).start()
    for t in range(tiles):
        pltpu.make_async_copy(buf.at[t], buf.at[t], sems.at[t]).wait()

    def leave(f, d):
        span = pl.ds(f * side, side + (NOTE if f == count - 1 else 0))
        return pltpu.make_async_copy(made.at[d, span], outs[d].at[span], out_sems.at[f, d])

    def block(place, f):
        at = slot_ref[place]
        row = pl.multiple_of((at % capacity) * rows + f * BPHI, BPHI)
        return scaled(buf[at // capacity, pl.ds(row, BPHI)], weight_ref[place])

    for f in range(count):
        for j in range(per_plane // 2):

            def body(g, carry):
                even = block(2 * j * CG_DEV + g, f)
                odd = block((2 * j + 1) * CG_DEV + g, f)
                x = jnp.concatenate([even, odd], axis=0).T
                to = pl.ds(pl.multiple_of(f * side + g * sliver, sliver), sliver)
                for p in range(planes):
                    distance = (p - me + planes) % planes
                    made[distance, to, pl.ds(j * LANES, LANES)] = x[p * sliver : (p + 1) * sliver]
                return carry

            lax.fori_loop(0, CG_DEV, body, 0, unroll=4)
        for d in range(planes):
            leave(f, d).start()
    for f in range(count):
        for d in range(planes):
            leave(f, d).wait()


def sort(arrived, slot, weight, note, me, planes, count, capacity):
    cells = slot.shape[0] // CG_DEV * BPHI
    rows = count * CG_DEV * (COLS // planes) + NOTE
    return pl.pallas_call(
        functools.partial(sort_kernel, planes, count, capacity),
        in_specs=[SMEM, SMEM, SMEM, VMEM, ANY],
        out_specs=[HBM] * planes,
        out_shape=[pltpu.HBM((rows, cells), jnp.bfloat16)] * planes,
        scratch_shapes=[
            pltpu.VMEM(arrived.shape, jnp.bfloat16),
            pltpu.VMEM((planes, rows, cells), jnp.bfloat16),
            pltpu.SemaphoreType.DMA((arrived.shape[0],)),
            pltpu.SemaphoreType.DMA((count, planes)),
        ],
        compiler_params=params(),
        cost_estimate=LIGHT,
        name="sort",
    )(me, slot, weight, note, *in_hbm(arrived))


def mail_kernel(planes, tiles, capacity, slot_ref, *refs):
    ins, (out_ref, box_ref, buf, sems, out_sems) = refs[:planes], refs[planes:]
    slots = slot_ref.shape[1]
    sliver = box_ref.shape[1] // (planes * capacity)
    for d in range(planes):
        source = ins[d].at[pl.ds(0, slots * sliver)]
        pltpu.make_async_copy(source, buf.at[d], sems.at[d]).start()
    for d in range(planes):
        pltpu.make_async_copy(buf.at[d], buf.at[d], sems.at[d]).wait()

        def body(i, carry):
            to = slot_ref[d, i]
            row = pl.multiple_of((to % (planes * capacity)) * sliver, sliver)
            source = pl.ds(pl.multiple_of(i * sliver, sliver), sliver)
            box_ref[to // (planes * capacity), pl.ds(row, sliver)] = buf[d, source]
            return carry

        lax.fori_loop(0, slots, body, 0, unroll=4)
    for t in range(tiles):
        pltpu.make_async_copy(box_ref.at[t], out_ref.at[t], out_sems.at[t]).start()
    for t in range(tiles):
        pltpu.make_async_copy(box_ref.at[t], out_ref.at[t], out_sems.at[t]).wait()


def mail(parts, slot, tiles, capacity):
    planes, slots = slot.shape
    sliver = COLS // planes
    rows = planes * capacity * sliver
    return pl.pallas_call(
        functools.partial(mail_kernel, planes, tiles, capacity),
        in_specs=[SMEM] + [ANY] * planes,
        out_specs=HBM,
        out_shape=pltpu.HBM((tiles, rows, LANES), jnp.bfloat16),
        scratch_shapes=[
            pltpu.VMEM((tiles, rows, LANES), jnp.bfloat16),
            pltpu.VMEM((planes, slots * sliver, LANES), jnp.bfloat16),
            pltpu.SemaphoreType.DMA((planes,)),
            pltpu.SemaphoreType.DMA((tiles,)),
        ],
        compiler_params=params(),
        cost_estimate=SLOW,
        name="mail",
    )(slot, *in_hbm(*parts))


def load_basis(basis_hbm, basis, sems, spans):
    for j in spans:
        pltpu.make_async_copy(basis_hbm.at[j], basis.at[j], sems.at[j]).start()


def multiply(order, basis, out_hbm, rows, acc, basis_sems, sems, beside=None):
    wide = acc.shape[-1]
    copies = []
    for f, field in enumerate(order):
        for j in range(SPANS):
            n = len(copies)
            if f == 0:
                pltpu.make_async_copy(basis.at[j], basis.at[j], basis_sems.at[j]).wait()
            if n >= 2:
                copies[n - 2].wait()
            if beside is not None:
                beside(n)
            acc[n % 2] = jnp.dot(
                rows[f][...], basis[j], preferred_element_type=jnp.float32
            ).reshape(acc.shape[1:])
            copy = pltpu.make_async_copy(
                acc.at[n % 2], out_hbm.at[field, :, :, pl.ds(j * wide, wide)], sems.at[n % 2]
            )
            copy.start()
            copies.append(copy)
    for copy in copies[-2:]:
        copy.wait()


def load_rows(ins, take, rows, sems):
    cells = ins[0].shape[1]
    side = rows.shape[0]
    for d in range(len(ins)):
        to = rows.at[:, pl.ds(d * cells, cells)]
        pltpu.make_async_copy(ins[d].at[pl.ds(take * side, side)], to, sems.at[d]).start()


def wait_rows(planes, rows, sems):
    cells = rows.shape[1] // planes
    for d in range(planes):
        to = rows.at[:, pl.ds(d * cells, cells)]
        pltpu.make_async_copy(to, to, sems.at[d]).wait()


def rows_kernel(planes, take, field, chained, *refs):
    ins, basis_hbm = refs[:planes], refs[planes]
    out_hbm, rows, basis, acc, in_sems, basis_sems, out_sems = refs[planes + 1 + chained :]
    load_rows(ins, take, rows, in_sems)
    load_basis(basis_hbm, basis, basis_sems, range(1))
    wait_rows(planes, rows, in_sems)
    load_basis(basis_hbm, basis, basis_sems, range(1, SPANS))
    multiply((field,), basis, out_hbm, (rows,), acc, basis_sems, out_sems)


def box_kernel(planes, per_plane, capacity, *refs):
    slot_ref, box_hbm, basis_hbm, _, out_hbm = refs[:5]
    one, two, basis, acc, box, box_sems, basis_sems, out_sems = refs[5:]
    tiles = box.shape[0]
    sliver = COLS // planes
    for t in range(tiles):
        pltpu.make_async_copy(box_hbm.at[t], box.at[t], box_sems.at[t]).start()
    load_basis(basis_hbm, basis, basis_sems, range(1))
    for t in range(tiles):
        pltpu.make_async_copy(box.at[t], box.at[t], box_sems.at[t]).wait()
    load_basis(basis_hbm, basis, basis_sems, range(1, SPANS))

    def piece(d, place):
        at = slot_ref[d, place]
        row = pl.multiple_of((at % (planes * capacity)) * sliver, sliver)
        return box[at // (planes * capacity), pl.ds(row, sliver)]

    def gather(rows, cells, d):
        for j in range(per_plane // 2):
            lanes = pl.ds((d * per_plane + 2 * j) * BPHI, LANES)
            for g in range(CG_DEV):
                even = piece(d, 2 * j * CG_DEV + g)
                odd = piece(d, (2 * j + 1) * CG_DEV + g)
                both = jnp.concatenate([even[:, cells], odd[:, cells]], axis=1)
                rows[pl.ds(g * sliver, sliver), lanes] = both

    def beside(n):
        for d in range(planes):
            if n == d * SPANS // planes:
                gather(two, slice(BPHI, LANES), d)

    for d in range(planes):
        gather(one, slice(0, BPHI), d)
    multiply(PAIR, basis, out_hbm, (one, two), acc, basis_sems, out_sems, beside)


def transform(kernel, operands, specs, total, basis, planes, fields, extra, sems, cost, name):
    sliver = COLS // planes
    operands = operands + in_hbm(basis)
    specs = specs + [ANY]
    aliases = {}
    if total is not None:
        aliases = {len(operands): 0}
        operands, specs = operands + [total], specs + [ANY]
    rows = pltpu.VMEM((CG_DEV * sliver, NPHI), jnp.bfloat16)
    return pl.pallas_call(
        kernel,
        in_specs=specs,
        out_specs=HBM,
        out_shape=pltpu.HBM((FIELDS, CG_DEV, sliver, NPHI), jnp.float32),
        scratch_shapes=[rows] * fields
        + [
            pltpu.VMEM((SPANS, NPHI, NPHI // SPANS), jnp.bfloat16),
            pltpu.VMEM((2, CG_DEV, sliver, NPHI // SPANS), jnp.float32),
        ]
        + extra
        + [pltpu.SemaphoreType.DMA((sems,))]
        + [pltpu.SemaphoreType.DMA((SPANS,)), pltpu.SemaphoreType.DMA((2,))],
        input_output_aliases=aliases,
        compiler_params=params(),
        cost_estimate=cost,
        name=name,
    )(*operands)


def transform_rows(slabs, take, basis, total, field, cost):
    planes = len(slabs)
    kernel = functools.partial(rows_kernel, planes, take, field, int(total is not None))
    operands, specs = list(slabs), [ANY] * planes
    return transform(kernel, operands, specs, total, basis, planes, 1, [], planes, cost, "rows")


def transform_box(box, slot, basis, total, per_plane, capacity):
    planes, tiles = slot.shape[0], box.shape[0]
    kernel = functools.partial(box_kernel, planes, per_plane, capacity)
    operands, specs = [slot] + in_hbm(box), [SMEM, ANY]
    extra = [pltpu.VMEM(box.shape, jnp.bfloat16)]
    return transform(kernel, operands, specs, total, basis, planes, 2, extra, tiles, LIGHT, "box")


def rank_of(dest):
    slots = dest.shape[-1]
    at = jnp.arange(slots, dtype=jnp.int32)
    same = (dest[..., :, None] == dest[..., None, :]) & (at[None, :] < at[:, None])
    return jnp.sum(same.astype(jnp.int32), axis=-1)


def as_note(dest, place_level, width):
    count = dest.size
    each = -(-count // width)
    row = jnp.arange(NOTE, dtype=jnp.int32)[:, None]
    if each > 1:
        codes = [c.reshape(-1) for c in (dest, place_level)]
        codes = [jnp.pad(c, (0, each * width - count)).reshape(each, width) for c in codes]
        both = jnp.concatenate(codes, axis=0)
        return jnp.pad(both, ((0, NOTE - 2 * each), (0, 0))).astype(jnp.bfloat16)
    wide = [jnp.pad(c.reshape(1, -1), ((0, 0), (0, width - count))) for c in (dest, place_level)]
    return jnp.where(row == 0, wide[0], jnp.where(row == 1, wide[1], 0)).astype(jnp.bfloat16)


def from_note(note, count):
    width = note.shape[2]
    each = -(-count // width)
    note = note.astype(jnp.float32).astype(jnp.int32)
    dest = note[:, :each].reshape(-1, each * width)[:, :count]
    place_level = note[:, each : 2 * each].reshape(-1, each * width)[:, :count]
    return dest, place_level


def local(blocks, levels, block_dest, block_phi, block_group):
    tiles = lax.axis_size("tile")
    planes = lax.axis_size("phi")
    tile = lax.axis_index("tile")
    plane = lax.axis_index("phi")
    slots = blocks.shape[0]
    per_plane = NPHI // BPHI // planes
    places = per_plane * CG_DEV
    capacity = 2 * slots // tiles
    me = plane.astype(jnp.int32).reshape(1)
    weight = 1.0 / jnp.left_shift(1, levels).astype(jnp.float32)
    place_iota = jnp.arange(places, dtype=jnp.int32)

    def over_phi(parts):
        moved = [parts[0]]
        for d in range(1, planes):
            pairs = [(s, (s + d) % planes) for s in range(planes)]
            moved.append(lax.ppermute(parts[d], "phi", pairs))
        return moved

    def over_tile(box):
        return lax.all_to_all(box, "tile", split_axis=0, concat_axis=0, tiled=True)

    def tie(value, *others):
        return lax.optimization_barrier((value,) + others)[0]

    place_level = levels * places + block_phi * CG_DEV + block_group
    distance = jnp.arange(planes, dtype=jnp.int32)[:, None]
    box_note = as_note(block_dest, place_level, COLS)
    box = post(blocks, block_dest, box_note, GROUPS[0], tiles, capacity, LIGHT)
    pieces = cut(blocks, weight, as_note(block_dest, place_level, LANES), me, planes)
    source = tie(blocks, pieces[0])
    next_box = post(source, block_dest, box_note, GROUPS[1], tiles, capacity, SLOWER)

    back = (plane - jnp.arange(planes, dtype=jnp.int32)) % planes
    basis = rotated_basis(NPHI, back)

    first = over_tile(box)
    sent = over_phi(pieces)
    second = over_tile(tie(next_box, first, basis))

    got_dest, got_code = from_note(first[:, -NOTE:], slots)
    got_slot = jnp.arange(tiles, dtype=jnp.int32)[:, None] * capacity + rank_of(got_dest)
    here = (got_dest == tile)[..., None] & ((got_code % places)[..., None] == place_iota)
    slot = jnp.sum(jnp.where(here, got_slot[..., None], 0), axis=(0, 1))
    level = jnp.sum(jnp.where(here, (got_code // places)[..., None], 0), axis=(0, 1))
    got_weight = 1.0 / jnp.left_shift(1, level).astype(jnp.float32)
    note = as_note(got_dest, got_code, per_plane * BPHI)

    early = sort(first, slot, got_weight, note, me, planes, 2, capacity)
    sent = list(lax.optimization_barrier((tuple(sent), early[0]))[0])
    early = over_phi(early)

    dest, _ = from_note(jnp.stack([part[-NOTE:] for part in sent]), slots)
    out_slot = (dest * planes + distance) * capacity + rank_of(dest)

    outbox = mail(sent, out_slot, tiles, capacity)
    last = over_tile(tie(outbox, second))
    rest = sort(second, slot, got_weight, note, me, planes, 1, capacity)
    early = [tie(early[0], *rest)] + early[1:]
    rest = over_phi(rest)

    from_dest, from_code = from_note(jnp.stack([part[-NOTE:] for part in early]), tiles * slots)
    from_dest = from_dest.reshape(planes, tiles, slots)
    from_place = from_code.reshape(planes, tiles, slots) % places
    start = jnp.arange(tiles, dtype=jnp.int32)[None, :, None] * planes + distance[..., None]
    from_slot = start * capacity + rank_of(from_dest)
    here = (from_dest == tile)[..., None] & (from_place[..., None] == place_iota)
    routed = jnp.sum(jnp.where(here, from_slot[..., None], 0), axis=(1, 2))

    total = transform_rows(early, 0, basis, None, GROUPS[0][0], SLOWER)
    total = transform_rows(early, 1, basis, total, GROUPS[0][1], SLOWER)
    total = transform_box(last, routed, basis, total, per_plane, capacity)
    return transform_rows(rest, 0, basis, total, GROUPS[1][0], LIGHT)


def solution(mesh):
    in_specs = (
        P(("tile", "phi"), None, None, None),
        P(("tile", "phi")),
        P(("tile", "phi")),
        P(("tile", "phi")),
        P(("tile", "phi")),
    )
    out_specs = P(None, "tile", "phi", None)
    return jax.shard_map(local, mesh=mesh, in_specs=in_specs, out_specs=out_specs, check_vma=False)
```
